128 devices in a mesh: replica: 8 (over z_hi, x), fsdp: 16 (over z_lo, y, core).
Axes of the slice: x: 4, y: 4, z: 4 (z_hi: 2, z_lo: 2; z = z_hi * 2 + z_lo), core: 2. Of those that a mesh axis runs over, the one named last changes fastest.
Arguments:
- step: int32 [1], replicated, may hold values from 0 to 999
- hidden_in: bfloat16 [8, 2048, 3072], P('replica', 'fsdp'), may hold values from -6 to 6
- cotangent: bfloat16 [8, 2048, 3072], P('replica', 'fsdp'), may hold values from -6 to 6
- norm_gain: bfloat16 [3072], replicated, may hold values from 0.5 to 1.5
- weights: bfloat16 [8, 3, 3072, 4096], P('replica', None, None, 'fsdp'), may hold values from -0.109375 to 0.109375
- adam_m: float32 [8, 3072, 4096], P('replica', None, 'fsdp'), may hold values from -0.046875 to 0.046875
- adam_v: float32 [8, 3072, 4096], P('replica', None, 'fsdp'), may hold values from 1e-06 to 0.0001
- global_frag: float32 [3072, 4096], P(None, 'fsdp'), may hold values from -0.109375 to 0.109375
- outer_mom: float32 [3072, 4096], P(None, 'fsdp'), may hold values from -0.15625 to 0.15625
Outputs:
- global_new: float32 [3072, 4096], P(None, 'fsdp')
- momentum_new: float32 [3072, 4096], P(None, 'fsdp')
- merged: bfloat16 [8, 3072, 4096], P('replica', None, 'fsdp')
The draws below stay inside these ranges and needn't reach their ends.
All inputs are finite; a program needn't handle non-finite values.
Results may differ from the reference program's by a relative error of at most 0.0047.
Values may be sent and summed in bfloat16 or wider, within the bound.
No kernel may reach another device: no remote copies, remote signals or barrier semaphores. Data moves between devices by JAX's collectives and lax.ppermute only.
A program may use at most 128 MiB of HBM per device.

```python
import math
import jax
import jax.numpy as jnp
from jax import lax

D = 3072
FF = 4096
TOKENS = 2048
N_REPLICA = 8


def steps_of(stream_key, dims, pieces, least, top_value):
    factor_of = 1.0
    for dim, shards_of in pieces:
        draws = jax.random.uniform(jax.random.fold_in(jax.random.fold_in(stream_key, 6), dim), (shards_of,), jnp.float32, least / len(pieces), top_value / len(pieces))
        factor_of = factor_of * jnp.repeat(jnp.exp(draws), dims[dim] // shards_of).reshape((-1,) + (1,) * (len(dims) - 1 - dim))
    return factor_of


def centred(stream_key, shape, spread, reach, split=(), kind=jnp.bfloat16):
    gain = steps_of(stream_key, shape, split, -0.22, 0.18) if split else 1.0
    drawn = jax.random.normal(stream_key, shape, jnp.float32) * spread * gain
    return jnp.minimum(jnp.maximum(drawn, -reach), reach).astype(kind)


def setup_inputs(seed: int = 0) -> dict:
    splits = jax.random.split(jax.random.key(seed), 10)
    return {
        "step": jax.random.randint(splits[0], (1,), 0, 1000).astype(jnp.int32),
        "hidden_in": centred(splits[1], (N_REPLICA, TOKENS, D), 1.0, 6.0, ((0, 8), (1, 16))),
        "cotangent": centred(splits[2], (N_REPLICA, TOKENS, D), 1.0, 6.0, ((0, 8), (1, 16))),
        "norm_gain": jnp.clip(1.0 + 0.1 * jax.random.normal(splits[3], (D,), jnp.float32), 0.5, 1.5).astype(jnp.bfloat16),
        "weights": centred(splits[4], (N_REPLICA, 3, D, FF), D ** -0.5, 0.109375, ((0, 8), (3, 16))),
        "adam_m": centred(splits[5], (N_REPLICA, D, FF), 0.003, 0.046875, ((0, 8), (2, 16)), jnp.float32),
        "adam_v": jnp.clip(jnp.exp(math.log(0.0001) - 4.6051702 * jax.random.uniform(splits[6], (N_REPLICA, D, FF), jnp.float32) ** steps_of(splits[6], (N_REPLICA, D, FF), ((0, 8), (2, 16)), -0.2, 0.2)), 9.999999974752427e-07, 0.0001),
        "global_frag": centred(splits[7], (D, FF), D ** -0.5, 0.109375, ((1, 16),), jnp.float32),
        "outer_mom": centred(splits[8], (D, FF), 0.01, 0.15625, ((1, 16),), jnp.float32),
    }


beta_one = 0.9
beta_two = 0.95
adam_eps = 1e-08
inner_lr = 0.02
outer_lr = 0.7
nesterov_mu = 0.9
mix_alpha = 0.5
norm_eps = 1e-05

def reference(step, hidden_in, cotangent, norm_gain, weights, adam_m, adam_v, global_frag, outer_mom):
    fragment = (step[0] % 3).astype(jnp.int32)
    delta_sum = jnp.zeros(global_frag.shape, jnp.float32)
    inner_list = []
    for replica_idx in range(N_REPLICA):
        w_all = weights[replica_idx]
        x_float = hidden_in[replica_idx].astype(jnp.float32)
        scale_rows = lax.rsqrt(lax.optimization_barrier(jnp.mean(x_float * x_float, axis=1, keepdims=True)) + norm_eps)
        normed = (x_float * scale_rows * norm_gain.astype(jnp.float32)).astype(jnp.bfloat16)
        cotan = cotangent[replica_idx]
        gate = jnp.dot(normed, w_all[0], preferred_element_type=jnp.float32)
        up_val = jnp.dot(normed, w_all[1], preferred_element_type=jnp.float32)
        gate_sig = jax.nn.sigmoid(gate)
        activated = gate * gate_sig
        hidden = (activated * up_val).astype(jnp.bfloat16)
        d_hidden = jnp.dot(cotan, w_all[2], preferred_element_type=jnp.float32)
        d_gate = (d_hidden * up_val * gate_sig * (1.0 + gate * (1.0 - gate_sig))).astype(jnp.bfloat16)
        d_up = (d_hidden * activated).astype(jnp.bfloat16)
        left = jnp.where(fragment == 2, cotan, normed)
        right = jnp.where(fragment == 0, d_gate, jnp.where(fragment == 1, d_up, hidden))
        grad = lax.dot_general(left, right, (((0,), (0,)), ((), ())), preferred_element_type=jnp.float32) / TOKENS
        w_frag = lax.dynamic_index_in_dim(w_all, fragment, 0, keepdims=False).astype(jnp.float32)
        moment_one = beta_one * adam_m[replica_idx] + (1.0 - beta_one) * grad
        moment_two = beta_two * adam_v[replica_idx] + (1.0 - beta_two) * grad * grad
        inner_list.append(w_frag - inner_lr * moment_one / (jnp.sqrt(moment_two) + adam_eps))
        delta_sum = delta_sum + (global_frag - w_frag)
    delta = delta_sum / N_REPLICA
    momentum_new = nesterov_mu * outer_mom + delta
    global_new = global_frag - outer_lr * (delta + nesterov_mu * momentum_new)
    merged = jnp.stack([(mix_alpha * w_inner + (1.0 - mix_alpha) * global_new).astype(jnp.bfloat16) for w_inner in inner_list])
    return (global_new, momentum_new, merged)
```

```python
import functools

import jax
import jax.numpy as jnp
from jax import lax
from jax.experimental import pallas as pl
from jax.experimental.pallas import tpu as pltpu
from jax.sharding import PartitionSpec as P

beta_one = 0.9
beta_two = 0.95
adam_eps = 1e-08
inner_lr = 0.02
outer_lr = 0.7
nesterov_mu = 0.9
mix_alpha = 0.5
norm_eps = 1e-05

WIRE_SCALE = float(2**18)

ANY = pl.BlockSpec(memory_space=pl.ANY)
VMEM = pl.BlockSpec(memory_space=pltpu.VMEM)
SMEM = pl.BlockSpec(memory_space=pltpu.SMEM)
MIB = 1024 * 1024


def fsdp_id(z, y, c):
    return (z % 2) * 8 + (y % 4) * 2 + c


def permutation(to):
    return [(fsdp_id(z, y, c), fsdp_id(*to(z, y, c))) for z in range(2) for y in range(4) for c in range(2)]


STRAIGHT = permutation(lambda z, y, c: (z, y + 1 - 2 * c, c))
CROSSED = permutation(lambda z, y, c: (z, y + 2 * c - 1, 1 - c))
OTHER_Z = permutation(lambda z, y, c: (z + 1, y, c))
SIBLING = permutation(lambda z, y, c: (z, y, 1 - c))


def replica_shift(k):
    return [(h * 4 + x, h * 4 + (x + k) % 4) for h in range(2) for x in range(4)]


OTHER_H = [(r, (r + 4) % 8) for r in range(8)]


def norm_kernel(x_ref, c_ref, g_ref, u_ref):
    rows = x_ref.shape[0]
    x = x_ref[...].astype(jnp.float32)
    scale = lax.rsqrt(jnp.mean(x * x, axis=1, keepdims=True) + norm_eps)
    u_ref[pl.ds(0, rows), :] = (x * scale * g_ref[...].astype(jnp.float32)).astype(jnp.bfloat16)
    u_ref[pl.ds(rows, rows), :] = c_ref[...]


def normed_and_cotangent(x, c, gain):
    rows, d = x.shape
    return pl.pallas_call(
        norm_kernel,
        out_shape=jax.ShapeDtypeStruct((2 * rows, d), jnp.bfloat16),
        in_specs=[VMEM, VMEM, VMEM],
        out_specs=VMEM,
        compiler_params=pltpu.CompilerParams(vmem_limit_bytes=16 * MIB),
        name="norm",
    )(x, c, gain.reshape(1, d))


def forward_kernel(count, frag_ref, *refs):
    blocks = refs[:count]
    w_own, w_sib, right_ref = refs[count : count + 3]
    n_s, c_s, w_s, gate_s, up_s, dh_s, sems = refs[count + 3 :]
    rows = blocks[0].shape[0] // 2
    cols = w_own.shape[2]
    frag = frag_ref[0]
    copies = []
    for k, block in enumerate(blocks):
        copies.append(pltpu.make_async_copy(block.at[pl.ds(0, rows)], n_s.at[pl.ds(k * rows, rows)], sems.at[2 * k]))
        copies.append(pltpu.make_async_copy(block.at[pl.ds(rows, rows)], c_s.at[pl.ds(k * rows, rows)], sems.at[2 * k + 1]))
    weights = [
        pltpu.make_async_copy(w.at[m], w_s.at[3 * h + m], sems.at[2 * count + 3 * h + m])
        for h, w in enumerate((w_own, w_sib))
        for m in range(3)
    ]
    for copy in copies + weights:
        copy.start()
    for copy in copies:
        copy.wait()
    for h in range(2):
        for m, (left, out) in enumerate(((n_s, gate_s), (n_s, up_s), (c_s, dh_s))):
            weights[3 * h + m].wait()
            out[...] = jnp.dot(left[...], w_s[3 * h + m], preferred_element_type=jnp.float32)
        gate = gate_s[...]
        sig = jax.nn.sigmoid(gate)
        at = right_ref.at[:, pl.ds(h * cols, cols)]

        @pl.when(frag == 0)
        def _():
            at[...] = (dh_s[...] * up_s[...] * sig * (1.0 + gate * (1.0 - sig))).astype(jnp.bfloat16)

        @pl.when(frag == 1)
        def _():
            at[...] = (dh_s[...] * (gate * sig)).astype(jnp.bfloat16)

        @pl.when(frag == 2)
        def _():
            at[...] = (gate * sig * up_s[...]).astype(jnp.bfloat16)


def forward(frag, blocks, w_own, w_sib):
    count = len(blocks)
    rows = count * blocks[0].shape[0] // 2
    _, d, cols = w_own.shape
    return pl.pallas_call(
        functools.partial(forward_kernel, count),
        out_shape=jax.ShapeDtypeStruct((rows, 2 * cols), jnp.bfloat16),
        in_specs=[SMEM] + [ANY] * (count + 2),
        out_specs=VMEM,
        scratch_shapes=[
            pltpu.VMEM((rows, d), jnp.bfloat16),
            pltpu.VMEM((rows, d), jnp.bfloat16),
            pltpu.VMEM((6, d, cols), jnp.bfloat16),
            pltpu.VMEM((rows, cols), jnp.float32),
            pltpu.VMEM((rows, cols), jnp.float32),
            pltpu.VMEM((rows, cols), jnp.float32),
            pltpu.SemaphoreType.DMA((2 * count + 6,)),
        ],
        compiler_params=pltpu.CompilerParams(vmem_limit_bytes=32 * MIB),
        cost_estimate=pl.CostEstimate(flops=12 * rows * d * cols, bytes_accessed=12 * d * cols + 4 * rows * d, transcendentals=0),
        name="forward",
    )(frag, *blocks, w_own, w_sib)


def grad_kernel(count, spans, chunk, frag_ref, *refs):
    blocks = refs[:count]
    rights = refs[count : count + len(spans)]
    sib_ref, own_ref, left_s, right_s, sems = refs[count + len(spans) :]
    rows = blocks[0].shape[0] // 2
    cols = own_ref.shape[1]
    start = jnp.where(frag_ref[0] == 2, rows, 0)
    start = pl.multiple_of(start, rows)
    copies = [
        pltpu.make_async_copy(block.at[pl.ds(start, rows)], left_s.at[pl.ds(k * rows, rows)], sems.at[k])
        for k, block in enumerate(blocks)
    ]
    copies += [
        pltpu.make_async_copy(r, right_s.at[pl.ds(at, size)], sems.at[count + j])
        for j, (r, (at, size)) in enumerate(zip(rights, spans))
    ]
    for copy in copies:
        copy.start()
    for copy in copies:
        copy.wait()
    for out, at in ((sib_ref, cols), (own_ref, 0)):

        @pl.loop(0, left_s.shape[1] // chunk)
        def _(j):
            span = pl.ds(pl.multiple_of(j * chunk, chunk), chunk)
            out[span, :] = lax.dot_general(
                left_s[:, span], right_s[:, pl.ds(at, cols)], (((0,), (0,)), ((), ())), preferred_element_type=jnp.float32
            ).astype(out.dtype)


def partial_grads(frag, blocks, rights):
    count = len(blocks)
    rows, d = blocks[0].shape
    rows //= 2
    cols = rights[0].shape[1] // 2
    spans, at = [], 0
    for r in rights:
        spans.append((at, r.shape[0]))
        at += r.shape[0]
    return pl.pallas_call(
        functools.partial(grad_kernel, count, tuple(spans), 256),
        out_shape=(jax.ShapeDtypeStruct((d, cols), jnp.bfloat16), jax.ShapeDtypeStruct((d, cols), jnp.float32)),
        in_specs=[SMEM] + [ANY] * (count + len(rights)),
        out_specs=(VMEM, VMEM),
        scratch_shapes=[
            pltpu.VMEM((at, d), jnp.bfloat16),
            pltpu.VMEM((at, 2 * cols), jnp.bfloat16),
            pltpu.SemaphoreType.DMA((count + len(rights),)),
        ],
        compiler_params=pltpu.CompilerParams(vmem_limit_bytes=32 * MIB),
        cost_estimate=pl.CostEstimate(flops=4 * at * d * cols, bytes_accessed=2 * at * d + 6 * d * cols, transcendentals=0),
        name="grad",
    )(frag, *blocks, *rights)


def replica_delta(w_frag, global_frag):
    x = lax.rem(lax.axis_index("replica"), 4)
    d, cols = w_frag.shape
    quarters = w_frag.reshape(4, d // 4, cols)

    def quarter(k):
        return lax.dynamic_index_in_dim(quarters, lax.rem(x + k, 4), 0, keepdims=False)

    got = [quarter(0)] + [lax.ppermute(quarter(k), "replica", replica_shift(k)) for k in (1, 2, 3)]
    base = lax.dynamic_index_in_dim(global_frag.reshape(4, d // 4, cols), x, 0, keepdims=False)
    part = sum(base - w.astype(jnp.float32) for w in got)
    part = (part * (WIRE_SCALE / 8)).astype(jnp.float16)
    other = lax.ppermute(part, "replica", OTHER_H)
    mine = (part.astype(jnp.float32) + other.astype(jnp.float32)).astype(jnp.float16)
    slots = [mine] + [lax.ppermute(mine, "replica", replica_shift(k)) for k in (1, 2, 3)]
    twice = jnp.stack([slots[(-j) % 4] for j in range(8)])
    return lax.dynamic_slice_in_dim(twice, lax.rem(4 - x, 4), 4, 0).reshape(d, cols)


def per_device(step, hidden_in, cotangent, norm_gain, weights, adam_m, adam_v, global_frag, outer_mom):
    fragment = step[0] % 3
    frag = fragment.reshape(1)
    w_own = weights[0]
    w_sib = lax.ppermute(w_own, "fsdp", SIBLING)
    own = normed_and_cotangent(hidden_in[0], cotangent[0], norm_gain)

    straight = functools.partial(lax.ppermute, axis_name="fsdp", perm=STRAIGHT)
    crossed = functools.partial(lax.ppermute, axis_name="fsdp", perm=CROSSED)
    other_z = functools.partial(lax.ppermute, axis_name="fsdp", perm=OTHER_Z)
    near = straight(own)
    cross = crossed(own)
    z_own = other_z(own)
    z_near = straight(z_own)
    far = straight(near)
    z_cross = other_z(cross)
    z_far = straight(z_near)

    w_frag = lax.dynamic_index_in_dim(w_own, fragment, 0, keepdims=False)
    delta = replica_delta(w_frag, global_frag).astype(jnp.float32) * (1 / WIRE_SCALE)
    momentum_new = nesterov_mu * outer_mom + delta
    global_new = global_frag - outer_lr * (delta + nesterov_mu * momentum_new)

    groups = ((own, near), (cross, z_own), (z_near, far), (z_cross, z_far))
    rights = [forward(frag, group, w_own, w_sib) for group in groups]
    grad_sib, grad_own = partial_grads(frag, sum(groups, ()), rights)
    tokens_total = hidden_in.shape[1] * lax.axis_size("fsdp")
    grad = (grad_own + lax.ppermute(grad_sib, "fsdp", SIBLING).astype(jnp.float32)) / tokens_total

    moment_one = beta_one * adam_m[0] + (1.0 - beta_one) * grad
    moment_two = beta_two * adam_v[0] + (1.0 - beta_two) * grad * grad
    w_inner = w_frag.astype(jnp.float32) - inner_lr * moment_one / (jnp.sqrt(moment_two) + adam_eps)
    merged = (mix_alpha * w_inner + (1.0 - mix_alpha) * global_new).astype(jnp.bfloat16)
    return (global_new, momentum_new, merged[None])


def solution(mesh):
    placed = (
        P(),
        P("replica", "fsdp", None),
        P("replica", "fsdp", None),
        P(),
        P("replica", None, None, "fsdp"),
        P("replica", None, "fsdp"),
        P("replica", None, "fsdp"),
        P(None, "fsdp"),
        P(None, "fsdp"),
    )
    return jax.shard_map(
        per_device,
        mesh=mesh,
        in_specs=placed,
        out_specs=(P(None, "fsdp"), P(None, "fsdp"), P("replica", None, "fsdp")),
        check_vma=False,
    )
```

```python
import functools

import jax
import jax.numpy as jnp
from jax import lax
from jax.experimental import pallas as pl
from jax.experimental.pallas import tpu as pltpu
from jax.sharding import PartitionSpec as P

beta_one = 0.9
beta_two = 0.95
adam_eps = 1e-08
inner_lr = 0.02
outer_lr = 0.7
nesterov_mu = 0.9
mix_alpha = 0.5
norm_eps = 1e-05

WIRE_SCALE = float(2**18)

ANY = pl.BlockSpec(memory_space=pl.ANY)
VMEM = pl.BlockSpec(memory_space=pltpu.VMEM)
SMEM = pl.BlockSpec(memory_space=pltpu.SMEM)
MIB = 1024 * 1024
CHEAP = pl.CostEstimate(flops=1, bytes_accessed=1, transcendentals=0)


def fsdp_id(z, y, c):
    return (z % 2) * 8 + (y % 4) * 2 + c


def permutation(to):
    return [(fsdp_id(z, y, c), fsdp_id(*to(z, y, c))) for z in range(2) for y in range(4) for c in range(2)]


STRAIGHT = permutation(lambda z, y, c: (z, y + 1 - 2 * c, c))
CROSSED = permutation(lambda z, y, c: (z, y + 2 * c - 1, 1 - c))
OTHER_Z = permutation(lambda z, y, c: (z + 1, y, c))
SIBLING = permutation(lambda z, y, c: (z, y, 1 - c))

HALF_PAIR = [(h * 4 + x, h * 4 + (x ^ 1)) for h in range(2) for x in range(4)]
QUARTER_PAIR = [(h * 4 + x, h * 4 + 3 - x) for h in range(2) for x in range(4)]
OTHER_H = [(r, (r + 4) % 8) for r in range(8)]


def norm_kernel(x_ref, c_ref, g_ref, u_ref):
    x = x_ref[...].astype(jnp.float32)
    scale = lax.rsqrt(jnp.mean(x * x, axis=1, keepdims=True) + norm_eps)
    gain = g_ref[...].astype(jnp.float32).reshape(1, -1)
    u_ref[0] = (x * scale * gain).astype(jnp.bfloat16)
    u_ref[1] = c_ref[...]


def normed_and_cotangent(x, c, gain):
    rows, d = x.shape
    tile = 32
    return pl.pallas_call(
        norm_kernel,
        grid=(rows // tile,),
        out_shape=jax.ShapeDtypeStruct((2, rows, d), jnp.bfloat16),
        in_specs=[
            pl.BlockSpec((tile, d), lambda i: (i, 0)),
            pl.BlockSpec((tile, d), lambda i: (i, 0)),
            pl.BlockSpec((d,), lambda i: (0,)),
        ],
        out_specs=pl.BlockSpec((2, tile, d), lambda i: (0, i, 0)),
        compiler_params=pltpu.CompilerParams(vmem_limit_bytes=60 * MIB),
        cost_estimate=CHEAP,
        name="norm",
    )(x, c, gain)


def blocks_kernel(count, past, halves, emit, has_total, frag_ref, *refs):
    def take(n):
        nonlocal refs
        taken, refs = refs[:n], refs[n:]
        return taken

    blocks, old_blocks, weights = take(count), take(past), take(halves)
    old_right = take(1)[0] if past else None
    totals = take(halves) if has_total else None
    outs = take(halves if emit else 1)
    n_s, c_s, w_s, up_s, dh_s, right_s, left_s, past_s, sems = refs
    rows = blocks[0].shape[1]
    cols = weights[0].shape[2]
    frag = frag_ref[0]
    used = 0

    def load(source, target):
        nonlocal used
        copy = pltpu.make_async_copy(source, target, sems.at[used])
        used += 1
        copy.start()
        return copy

    def load_weight(h, m):
        return load(weights[h].at[m], w_s.at[3 * h + m])

    n_in = [load(b.at[0], n_s.at[pl.ds(k * rows, rows)]) for k, b in enumerate(blocks)]
    w_in = [load_weight(0, 0), load_weight(0, 1)]
    c_in = [load(b.at[1], c_s.at[pl.ds(k * rows, rows)]) for k, b in enumerate(blocks)]
    w_in += [load_weight(0, 2)] + [load_weight(h, m) for h in range(1, halves) for m in range(3)]
    side = jnp.where(frag == 2, 1, 0)
    old_in = [load(b.at[side], left_s.at[pl.ds(k * rows, rows)]) for k, b in enumerate(old_blocks)]
    if past:
        old_in.append(load(old_right, past_s))

    def dot(left, i):
        return jnp.dot(left[...], w_s[i], preferred_element_type=jnp.float32)

    def times(left_t, right):
        return jnp.dot(left_t, right, preferred_element_type=jnp.float32)

    for copy in n_in:
        copy.wait()
    for h in range(halves):
        w_in[3 * h].wait()
        gate = dot(n_s, 3 * h)
        w_in[3 * h + 1].wait()

        @pl.when(frag != 1)
        def _():
            up_s[...] = dot(n_s, 3 * h + 1)

        if h == 0:
            for copy in c_in:
                copy.wait()
        w_in[3 * h + 2].wait()

        @pl.when(frag != 2)
        def _():
            dh_s[...] = dot(c_s, 3 * h + 2)

        sig = jax.nn.sigmoid(gate)
        here = slice(h * cols, (h + 1) * cols)
        right = right_s if emit else outs[0].at[:, here]

        @pl.when(frag == 0)
        def _():
            right[...] = (dh_s[...] * up_s[...] * sig * (1.0 + gate * (1.0 - sig))).astype(jnp.bfloat16)

        @pl.when(frag == 1)
        def _():
            right[...] = (dh_s[...] * (gate * sig)).astype(jnp.bfloat16)

        @pl.when(frag == 2)
        def _():
            right[...] = (gate * sig * up_s[...]).astype(jnp.bfloat16)

        if not emit:
            continue
        if h == 0:
            for copy in old_in:
                copy.wait()

        right_t = right_s[...].T
        past_t = past_s[:, here].T if past else None

        def add(left):
            step = 768
            for at in range(0, left.shape[1], step):
                span = slice(at, at + step)
                term = times(right_t, left[:, span])
                if past:
                    term = term + times(past_t, left_s[:, span])
                if has_total:
                    term = term + totals[h][:, span]
                outs[h][:, span] = term.astype(outs[h].dtype)

        pl.when(frag == 2)(lambda: add(c_s))
        pl.when(frag != 2)(lambda: add(n_s))


def blocks_call(frag, blocks, weights, limit, old_blocks=(), old_right=None, totals=(), kind=None):
    count, past, halves = len(blocks), len(old_blocks), len(weights)
    rows = count * blocks[0].shape[1]
    past_rows = max(past * blocks[0].shape[1], 16)
    _, d, cols = weights[0].shape
    aliases = {}
    if totals and kind == jnp.float32:
        aliases = {1 + count + past + halves + bool(past) + h: h for h in range(halves)}
    if kind:
        outs = [jax.ShapeDtypeStruct((cols, d), kind)] * halves
    else:
        outs = [jax.ShapeDtypeStruct((rows, halves * cols), jnp.bfloat16)]
    operands = [frag, *blocks, *old_blocks, *weights] + ([old_right] if past else []) + list(totals)
    return pl.pallas_call(
        functools.partial(blocks_kernel, count, past, halves, bool(kind), bool(totals)),
        out_shape=outs,
        in_specs=[SMEM] + [ANY] * (len(operands) - 1 - len(totals)) + [VMEM] * len(totals),
        out_specs=[VMEM] * len(outs),
        scratch_shapes=[
            pltpu.VMEM((rows, d), jnp.bfloat16),
            pltpu.VMEM((rows, d), jnp.bfloat16),
            pltpu.VMEM((3 * halves, d, cols), jnp.bfloat16),
            pltpu.VMEM((rows, cols), jnp.float32),
            pltpu.VMEM((rows, cols), jnp.float32),
            pltpu.VMEM((rows if kind else 16, cols), jnp.bfloat16),
            pltpu.VMEM((past_rows, d), jnp.bfloat16),
            pltpu.VMEM((past_rows, halves * cols), jnp.bfloat16),
            pltpu.SemaphoreType.DMA((2 * count + 3 * halves + past + 1,)),
        ],
        input_output_aliases=aliases,
        compiler_params=pltpu.CompilerParams(vmem_limit_bytes=limit * MIB),
        cost_estimate=CHEAP,
        name="blocks",
    )(*operands)


def adam_kernel(tokens, own_ref, other_ref, m_ref, v_ref, mixed_ref, out_ref):
    grad = (own_ref[...] + other_ref[...].astype(jnp.float32)).T * (1.0 / tokens)
    moment_one = beta_one * m_ref[...] + (1.0 - beta_one) * grad
    moment_two = beta_two * v_ref[...] + (1.0 - beta_two) * grad * grad
    step_inner = inner_lr * moment_one / (jnp.sqrt(moment_two) + adam_eps)
    out_ref[...] = (mixed_ref[...] - mix_alpha * step_inner).astype(jnp.bfloat16)


def adam(tokens, own, other, m, v, mixed):
    d, cols = m.shape
    tile = 512
    wide = pl.BlockSpec((cols, tile), lambda i: (0, i))
    tall = pl.BlockSpec((tile, cols), lambda i: (i, 0))
    return pl.pallas_call(
        functools.partial(adam_kernel, tokens),
        grid=(d // tile,),
        out_shape=jax.ShapeDtypeStruct((d, cols), jnp.bfloat16),
        in_specs=[wide, wide, tall, tall, tall],
        out_specs=tall,
        compiler_params=pltpu.CompilerParams(vmem_limit_bytes=16 * MIB),
        cost_estimate=CHEAP,
        name="adam",
    )(own, other, m, v, mixed)


def after(value, *others):
    return lax.optimization_barrier((value, *others))[0]


def per_device(step, hidden_in, cotangent, norm_gain, weights, adam_m, adam_v, global_frag, outer_mom):
    fragment = step[0] % 3
    frag = fragment.reshape(1)
    w_own = weights[0]
    w_sib = lax.ppermute(w_own, "fsdp", SIBLING)
    w_both = [w_sib, w_own]
    own = normed_and_cotangent(hidden_in[0], cotangent[0], norm_gain)

    straight = functools.partial(lax.ppermute, axis_name="fsdp", perm=STRAIGHT)
    crossed = functools.partial(lax.ppermute, axis_name="fsdp", perm=CROSSED)
    other_z = functools.partial(lax.ppermute, axis_name="fsdp", perm=OTHER_Z)

    x = lax.rem(lax.axis_index("replica"), 4)
    h = lax.rem((x + 1) // 2, 2)
    q = x // 2
    d, cols = global_frag.shape
    half, quarter = d // 2, d // 4

    def w_rows(at, size):
        return lax.dynamic_slice(w_own, (fragment, at, 0), (1, size, cols))[0]

    def g_rows(at, size):
        return lax.dynamic_slice(global_frag, (at, 0), (size, cols))

    def wire(value):
        return (value * (WIRE_SCALE / 8)).astype(jnp.float16)

    near = straight(own)
    z_own = other_z(own)
    cross = crossed(own)
    w_pair = lax.ppermute(after(w_rows((1 - h) * half, half), own), "replica", HALF_PAIR)

    def pair_delta(at):
        base = g_rows(h * half + at, quarter)
        mine = w_rows(h * half + at, quarter).astype(jnp.float32)
        theirs = lax.dynamic_slice_in_dim(w_pair, at, quarter).astype(jnp.float32)
        return (base - mine) + (base - theirs)

    sent = wire(pair_delta((1 - q) * quarter))
    got = lax.ppermute(sent, "replica", QUARTER_PAIR)
    part = wire(pair_delta(q * quarter) + got.astype(jnp.float32) * (8 / WIRE_SCALE))
    part = after(part, near, cross, z_own)
    other = lax.ppermute(part, "replica", OTHER_H)

    z_near = straight(z_own)
    z_cross = other_z(cross)
    first = [own, near, cross, z_own]
    (right,) = blocks_call(frag, first, w_both, 58)
    far = straight(near)
    mine = (part.astype(jnp.float32) + other.astype(jnp.float32)).astype(jnp.float16)
    mine = after(mine, right)
    got = lax.ppermute(mine, "replica", QUARTER_PAIR)
    mine = jnp.where(q == 0, jnp.concatenate([mine, got]), jnp.concatenate([got, mine]))
    got = lax.ppermute(mine, "replica", HALF_PAIR)
    z_far = straight(after(z_near, right))

    delta = jnp.where(h == 0, jnp.concatenate([mine, got]), jnp.concatenate([got, mine]))
    delta = delta.astype(jnp.float32) * (1 / WIRE_SCALE)
    momentum_new = nesterov_mu * outer_mom + delta
    global_new = global_frag - outer_lr * (delta + nesterov_mu * momentum_new)
    mixed = mix_alpha * w_rows(0, d).astype(jnp.float32) + (1.0 - mix_alpha) * global_new

    second = [far, z_near, z_cross]
    totals = blocks_call(frag, second, w_both, 54, first, right, kind=jnp.float32)
    z_far = after(z_far, mixed, *totals)
    (grad_sib,) = blocks_call(frag, [z_far], [w_sib], 28, totals=totals[:1], kind=jnp.bfloat16)
    grad_sib = lax.ppermute(grad_sib, "fsdp", SIBLING)
    (grad_own,) = blocks_call(frag, [z_far], [w_own], 28, totals=totals[1:], kind=jnp.float32)
    tokens_total = hidden_in.shape[1] * lax.axis_size("fsdp")
    merged = adam(tokens_total, grad_own, grad_sib, adam_m[0], adam_v[0], mixed)
    return (global_new, momentum_new, merged[None])


def solution(mesh):
    placed = (
        P(),
        P("replica", "fsdp", None),
        P("replica", "fsdp", None),
        P(),
        P("replica", None, None, "fsdp"),
        P("replica", None, "fsdp"),
        P("replica", None, "fsdp"),
        P(None, "fsdp"),
        P(None, "fsdp"),
    )
    return jax.shard_map(
        per_device,
        mesh=mesh,
        in_specs=placed,
        out_specs=(P(None, "fsdp"), P(None, "fsdp"), P("replica", None, "fsdp")),
        check_vma=False,
    )
```

```python
import functools

import jax
import jax.numpy as jnp
from jax import lax
from jax.experimental import pallas as pl
from jax.experimental.pallas import tpu as pltpu
from jax.sharding import PartitionSpec as P

beta_one = 0.9
beta_two = 0.95
adam_eps = 1e-08
inner_lr = 0.02
outer_lr = 0.7
nesterov_mu = 0.9
mix_alpha = 0.5
norm_eps = 1e-05

WIRE_SCALE = float(2**18)

ANY = pl.BlockSpec(memory_space=pl.ANY)
VMEM = pl.BlockSpec(memory_space=pltpu.VMEM)
SMEM = pl.BlockSpec(memory_space=pltpu.SMEM)
MIB = 1024 * 1024
CHEAP = pl.CostEstimate(flops=1, bytes_accessed=1, transcendentals=0)


def fsdp_id(z, y, c):
    return (z % 2) * 8 + (y % 4) * 2 + c


def permutation(to):
    return [(fsdp_id(z, y, c), fsdp_id(*to(z, y, c))) for z in range(2) for y in range(4) for c in range(2)]


STRAIGHT = permutation(lambda z, y, c: (z, y + 1 - 2 * c, c))
CROSSED = permutation(lambda z, y, c: (z, y + 2 * c - 1, 1 - c))
OTHER_Z = permutation(lambda z, y, c: (z + 1, y, c))
SIBLING = permutation(lambda z, y, c: (z, y, 1 - c))


def replica_pairs(first):
    pairs = []
    for r in range(8):
        for i in range(16):
            beside = (r % 4) ^ 1 if (i % 2 == 0) == first else 3 - r % 4
            pairs.append((r * 16 + i, (r // 4 * 4 + beside) * 16 + i))
    return pairs


HALF_PAIR = replica_pairs(True)
QUARTER_PAIR = replica_pairs(False)
OPPOSITE = [(r, r // 4 * 4 + (r + 2) % 4) for r in range(8)]
OTHER_H = [(r, (r + 4) % 8) for r in range(8)]


def norm_kernel(x_ref, c_ref, g_ref, u_ref, x_s, g_s, sems):
    g_in = pltpu.make_async_copy(g_ref, g_s, sems.at[0])
    x_in = pltpu.make_async_copy(x_ref, x_s, sems.at[1])
    c_in = pltpu.make_async_copy(c_ref, u_ref.at[1], sems.at[2])
    for copy in (g_in, x_in, c_in):
        copy.start()
    g_in.wait()
    gain = g_s[...].astype(jnp.float32).reshape(1, -1)
    x_in.wait()
    x = x_s[...].astype(jnp.float32)
    scale = lax.rsqrt(jnp.mean(x * x, axis=1, keepdims=True) + norm_eps)
    u_ref[0] = (x * scale * gain).astype(jnp.bfloat16)
    c_in.wait()


def normed_and_cotangent(x, c, gain):
    return pl.pallas_call(
        norm_kernel,
        out_shape=jax.ShapeDtypeStruct((2, *x.shape), jnp.bfloat16),
        in_specs=[ANY, ANY, ANY],
        out_specs=VMEM,
        scratch_shapes=[
            pltpu.VMEM(x.shape, jnp.bfloat16),
            pltpu.VMEM(gain.shape, jnp.bfloat16),
            pltpu.SemaphoreType.DMA((3,)),
        ],
        compiler_params=pltpu.CompilerParams(vmem_limit_bytes=60 * MIB),
        cost_estimate=CHEAP,
        name="norm",
    )(x, c, gain)


class Loads:
    def __init__(self, frag, sems, ahead):
        self.frag, self.sems, self.ahead = frag, sems, ahead
        self.entries, self.started, self.waited = [], 0, 0

    def add(self, name, source, target, without=None):
        copy = pltpu.make_async_copy(source, target, self.sems.at[len(self.entries)])
        self.entries.append((name, copy, without))

    def unless(self, without, act):
        if without is None:
            act()
        else:
            pl.when(self.frag != without)(act)

    def start(self):
        while self.started < min(self.waited + self.ahead, len(self.entries)):
            _, copy, without = self.entries[self.started]
            self.unless(without, copy.start)
            self.started += 1

    def wait(self, name):
        while self.waited < len(self.entries) and self.entries[self.waited][0] == name:
            _, copy, without = self.entries[self.waited]
            self.unless(without, copy.wait)
            self.waited += 1
            self.start()


def right_side(frag, loads, tag, n_s, c_s, w_s, up_s, dh_s, right):
    def dot(left, i):
        return jnp.dot(left[...], w_s[i], preferred_element_type=jnp.float32)

    loads.wait(("n", tag))
    loads.wait(("gate", tag))
    gate = dot(n_s, 0)
    loads.wait(("up", tag))

    @pl.when(frag != 1)
    def _():
        up_s[...] = dot(n_s, 1)

    loads.wait(("c", tag))
    loads.wait(("down", tag))

    @pl.when(frag != 2)
    def _():
        dh_s[...] = dot(c_s, 2)

    sig = jax.nn.sigmoid(gate)

    @pl.when(frag == 0)
    def _():
        right[...] = (dh_s[...] * up_s[...] * sig * (1.0 + gate * (1.0 - sig))).astype(jnp.bfloat16)

    @pl.when(frag == 1)
    def _():
        right[...] = (dh_s[...] * (gate * sig)).astype(jnp.bfloat16)

    @pl.when(frag == 2)
    def _():
        right[...] = (gate * sig * up_s[...]).astype(jnp.bfloat16)


def forward_kernel(count, frag_ref, *refs):
    blocks, weights, out_ref = refs[:count], refs[count : count + 2], refs[count + 2]
    n_s, c_s, w_s, up_s, dh_s, sems = refs[count + 3 :]
    rows, cols = blocks[0].shape[1], weights[0].shape[2]
    frag = frag_ref[0]
    loads = Loads(frag, sems, count + 4)
    for h, weight in enumerate(weights):
        if h == 0:
            for k, b in enumerate(blocks):
                loads.add(("n", h), b.at[0], n_s.at[pl.ds(k * rows, rows)])
        loads.add(("gate", h), weight.at[0], w_s.at[h, 0])
        loads.add(("up", h), weight.at[1], w_s.at[h, 1], 1)
        if h == 0:
            for k, b in enumerate(blocks):
                loads.add(("c", h), b.at[1], c_s.at[pl.ds(k * rows, rows)], 2)
        loads.add(("down", h), weight.at[2], w_s.at[h, 2], 2)
    loads.start()
    for h in range(2):
        right = out_ref.at[:, h * cols : (h + 1) * cols]
        right_side(frag, loads, h, n_s, c_s, w_s.at[h], up_s, dh_s, right)


def forward(frag, blocks, weights):
    count, rows = len(blocks), len(blocks) * blocks[0].shape[1]
    _, d, cols = weights[0].shape
    return pl.pallas_call(
        functools.partial(forward_kernel, count),
        out_shape=jax.ShapeDtypeStruct((rows, 2 * cols), jnp.bfloat16),
        in_specs=[SMEM] + [ANY] * (count + 2),
        out_specs=VMEM,
        scratch_shapes=[
            pltpu.VMEM((rows, d), jnp.bfloat16),
            pltpu.VMEM((rows, d), jnp.bfloat16),
            pltpu.VMEM((2, 3, d, cols), jnp.bfloat16),
            pltpu.VMEM((rows, cols), jnp.float32),
            pltpu.VMEM((rows, cols), jnp.float32),
            pltpu.SemaphoreType.DMA((2 * count + 6,)),
        ],
        compiler_params=pltpu.CompilerParams(vmem_limit_bytes=60 * MIB),
        cost_estimate=CHEAP,
        name="forward",
    )(frag, *blocks, *weights)


def add_gradient(right_t, left, out, total=None):
    step = 768
    for at in range(0, out.shape[1], step):
        span = slice(at, at + step)
        term = jnp.dot(right_t, left[:, span], preferred_element_type=jnp.float32)
        if total is not None:
            term = total[:, span] + term
        out[:, span] = term.astype(out.dtype)


def gradient_kernel(past, spans, frag_ref, block, *refs):
    old_blocks, rights, refs = refs[:past], refs[past : past + len(spans)], refs[past + len(spans) :]
    weights, held, outs = refs[:2], refs[2:4], refs[4:6]
    n_s, c_s, up_s, dh_s, left_s, right_s, sems = refs[6:]
    rows, cols = block.shape[1], weights[0].shape[2]
    frag = frag_ref[0]
    side = jnp.where(frag == 2, 1, 0)
    loads = Loads(frag, sems, 8)
    for h in range(2):
        if h == 0:
            loads.add(("n", h), block.at[0], n_s)
        loads.add(("gate", h), weights[h].at[0], held[h].at[0])
        loads.add(("up", h), weights[h].at[1], held[h].at[1], 1)
        if h == 0:
            loads.add(("c", h), block.at[1], c_s)
        loads.add(("down", h), weights[h].at[2], held[h].at[2], 2)
        if h == 0:
            for right, (at, size) in zip(rights, spans):
                loads.add("rest", right, right_s.at[pl.ds(at, size)])
            for k, b in enumerate((*old_blocks, block)):
                loads.add("rest", b.at[side], left_s.at[pl.ds(k * rows, rows)])
    loads.start()
    for h in range(2):
        here = slice(h * cols, (h + 1) * cols)
        right_side(frag, loads, h, n_s, c_s, held[h], up_s, dh_s, right_s.at[past * rows :, here])
        loads.wait("rest")
        add_gradient(right_s[:, here].T, left_s, outs[h])


def gradients(frag, block, weights, old_blocks, rights):
    past, rows = len(old_blocks), block.shape[1]
    _, d, cols = weights[0].shape
    spans, at = [], 0
    for right in rights:
        spans.append((at, right.shape[0]))
        at += right.shape[0]
    total = at + rows
    out = pl.pallas_call(
        functools.partial(gradient_kernel, past, tuple(spans)),
        out_shape=[jax.ShapeDtypeStruct((3, d, cols), jnp.bfloat16)] * 2 + [jax.ShapeDtypeStruct((cols, d), jnp.float32)] * 2,
        in_specs=[SMEM] + [ANY] * (past + len(spans) + 3),
        out_specs=[VMEM] * 4,
        scratch_shapes=[
            pltpu.VMEM((rows, d), jnp.bfloat16),
            pltpu.VMEM((rows, d), jnp.bfloat16),
            pltpu.VMEM((rows, cols), jnp.float32),
            pltpu.VMEM((rows, cols), jnp.float32),
            pltpu.VMEM((total, d), jnp.bfloat16),
            pltpu.VMEM((total, 2 * cols), jnp.bfloat16),
            pltpu.SemaphoreType.DMA((past + len(spans) + 9,)),
        ],
        compiler_params=pltpu.CompilerParams(vmem_limit_bytes=20 * MIB),
        cost_estimate=CHEAP,
        name="gradients",
    )(frag, block, *old_blocks, *rights, *weights)
    return out[:2], out[2:]


def step_kernel(halves, frag_ref, block, *refs):
    weights, totals, outs = refs[:halves], refs[halves : 2 * halves], refs[2 * halves : 3 * halves]
    n_s, c_s, up_s, dh_s, right_s, sems = refs[3 * halves :]
    frag = frag_ref[0]
    loads = Loads(frag, sems, 2)
    loads.add(("n", 0), block.at[0], n_s)
    loads.add(("c", 0), block.at[1], c_s)
    loads.start()
    for h in range(halves):
        right_side(frag, loads, h, n_s, c_s, weights[h], up_s, dh_s, right_s)
        right_t = right_s[...].T
        pl.when(frag == 2)(functools.partial(add_gradient, right_t, c_s, outs[h], totals[h]))
        pl.when(frag != 2)(functools.partial(add_gradient, right_t, n_s, outs[h], totals[h]))


def add_block(frag, block, weights, totals, kind=jnp.float32):
    halves, rows = len(weights), block.shape[1]
    _, d, cols = weights[0].shape
    aliases = {2 + halves + h: h for h in range(halves)} if kind == jnp.float32 else {}
    return pl.pallas_call(
        functools.partial(step_kernel, halves),
        out_shape=[jax.ShapeDtypeStruct((cols, d), kind)] * halves,
        in_specs=[SMEM, ANY] + [VMEM] * (2 * halves),
        out_specs=[VMEM] * halves,
        scratch_shapes=[
            pltpu.VMEM((rows, d), jnp.bfloat16),
            pltpu.VMEM((rows, d), jnp.bfloat16),
            pltpu.VMEM((rows, cols), jnp.float32),
            pltpu.VMEM((rows, cols), jnp.float32),
            pltpu.VMEM((rows, cols), jnp.bfloat16),
            pltpu.SemaphoreType.DMA((2,)),
        ],
        input_output_aliases=aliases,
        compiler_params=pltpu.CompilerParams(vmem_limit_bytes=12 * MIB),
        cost_estimate=CHEAP,
        name="block",
    )(frag, block, *weights, *totals)


def adam_kernel(tokens, tile, own_ref, other_ref, m_ref, v_ref, mixed_ref, out_ref, out_s, sems):
    copies = []
    for i in range(m_ref.shape[0] // tile):
        span = slice(i * tile, (i + 1) * tile)
        grad = (own_ref[:, span] + other_ref[:, span].astype(jnp.float32)).T * (1.0 / tokens)
        moment_one = beta_one * m_ref[span, :] + (1.0 - beta_one) * grad
        moment_two = beta_two * v_ref[span, :] + (1.0 - beta_two) * grad * grad
        step_inner = inner_lr * moment_one / (jnp.sqrt(moment_two) + adam_eps)
        out_s[span, :] = (mixed_ref[span, :] - mix_alpha * step_inner).astype(jnp.bfloat16)
        copy = pltpu.make_async_copy(out_s.at[span, :], out_ref.at[span, :], sems.at[i])
        copy.start()
        copies.append(copy)
    for copy in copies:
        copy.wait()


def adam(tokens, own, other, m, v, mixed):
    d, cols = m.shape
    tile = 512
    return pl.pallas_call(
        functools.partial(adam_kernel, tokens, tile),
        out_shape=jax.ShapeDtypeStruct((d, cols), jnp.bfloat16),
        in_specs=[VMEM] * 5,
        out_specs=ANY,
        scratch_shapes=[pltpu.VMEM((d, cols), jnp.bfloat16), pltpu.SemaphoreType.DMA((d // tile,))],
        compiler_params=pltpu.CompilerParams(vmem_limit_bytes=12 * MIB),
        cost_estimate=CHEAP,
        name="adam",
    )(own, other, m, v, mixed)


def after(value, *others):
    return lax.optimization_barrier((value, *others))[0]


def per_device(step, hidden_in, cotangent, norm_gain, weights, adam_m, adam_v, global_frag, outer_mom):
    fragment = step[0] % 3
    frag = fragment.reshape(1)
    w_own = weights[0]
    w_sib = lax.ppermute(w_own, "fsdp", SIBLING)
    w_both = [w_sib, w_own]
    own = normed_and_cotangent(hidden_in[0], cotangent[0], norm_gain)

    straight = functools.partial(lax.ppermute, axis_name="fsdp", perm=STRAIGHT)
    crossed = functools.partial(lax.ppermute, axis_name="fsdp", perm=CROSSED)
    other_z = functools.partial(lax.ppermute, axis_name="fsdp", perm=OTHER_Z)

    x = lax.rem(lax.axis_index("replica"), 4)
    first_core = lax.rem(lax.axis_index("fsdp"), 2) == 0
    inner, upper = lax.rem((x + 1) // 2, 2), x // 2
    h = jnp.where(first_core, inner, upper)
    q = jnp.where(first_core, upper, inner)
    everyone = ("replica", "fsdp")
    d, cols = global_frag.shape
    half, quarter = d // 2, d // 4

    def w_rows(at, size):
        return lax.dynamic_slice(w_own, (fragment, at, 0), (1, size, cols))[0]

    def g_rows(at, size):
        return lax.dynamic_slice(global_frag, (at, 0), (size, cols))

    def ordered(second, first, other):
        return jnp.where(second == 0, jnp.concatenate([first, other]), jnp.concatenate([other, first]))

    def wire(value):
        return (value * (WIRE_SCALE / 8)).astype(jnp.float16)

    near = straight(own)
    z_own = other_z(own)
    cross = crossed(own)
    w_pair = lax.ppermute(after(w_rows((1 - h) * half, half), own), everyone, HALF_PAIR)

    def pair_delta(at):
        base = g_rows(h * half + at, quarter)
        mine = w_rows(h * half + at, quarter).astype(jnp.float32)
        theirs = lax.dynamic_slice_in_dim(w_pair, at, quarter).astype(jnp.float32)
        return (base - mine) + (base - theirs)

    sent = wire(pair_delta((1 - q) * quarter))
    got = lax.ppermute(sent, everyone, QUARTER_PAIR)
    part = wire(pair_delta(q * quarter) + got.astype(jnp.float32) * (8 / WIRE_SCALE))
    z_own, near, part = lax.optimization_barrier((z_own, near, part))
    other = lax.ppermute(part, "replica", OTHER_H)
    z_near = straight(z_own)
    far = straight(near)
    first = [own, near, cross, z_own]
    right = forward(frag, first, w_both)
    other = after(other, right)
    mine = (part.astype(jnp.float32) + other.astype(jnp.float32)).astype(jnp.float16)
    cross, mine = lax.optimization_barrier((cross, mine))
    z_cross = other_z(cross)
    beside, across = lax.ppermute(mine, everyone, QUARTER_PAIR), lax.ppermute(mine, everyone, HALF_PAIR)
    opposite = lax.ppermute(mine, "replica", OPPOSITE)
    z_near = after(z_near, beside)
    z_far = straight(z_near)
    rights = [right, forward(frag, [z_near], w_both)]

    delta = ordered(h, ordered(q, mine, beside), ordered(q, across, opposite)).astype(jnp.float32) * (1 / WIRE_SCALE)
    momentum_new = nesterov_mu * outer_mom + delta
    global_new = global_frag - outer_lr * (delta + nesterov_mu * momentum_new)
    mixed = mix_alpha * w_rows(0, d).astype(jnp.float32) + (1.0 - mix_alpha) * global_new

    held, totals = gradients(frag, after(far, mixed), w_both, [*first, z_near], rights)
    totals = add_block(frag, z_cross, held, totals)
    (grad_sib,) = add_block(frag, z_far, held[:1], totals[:1], jnp.bfloat16)
    grad_sib = lax.ppermute(grad_sib, "fsdp", SIBLING)
    (grad_own,) = add_block(frag, z_far, held[1:], totals[1:])
    tokens_total = hidden_in.shape[1] * lax.axis_size("fsdp")
    merged = adam(tokens_total, grad_own, grad_sib, adam_m[0], adam_v[0], mixed)
    return (global_new, momentum_new, merged[None])


def solution(mesh):
    placed = (
        P(),
        P("replica", "fsdp", None),
        P("replica", "fsdp", None),
        P(),
        P("replica", None, None, "fsdp"),
        P("replica", None, "fsdp"),
        P("replica", None, "fsdp"),
        P(None, "fsdp"),
        P(None, "fsdp"),
    )
    return jax.shard_map(
        per_device,
        mesh=mesh,
        in_specs=placed,
        out_specs=(P(None, "fsdp"), P(None, "fsdp"), P("replica", None, "fsdp")),
        check_vma=False,
    )
```

```python
import functools

import jax
import jax.numpy as jnp
from jax import lax
from jax.experimental import pallas as pl
from jax.experimental.pallas import tpu as pltpu
from jax.sharding import PartitionSpec as P

beta_one = 0.9
beta_two = 0.95
adam_eps = 1e-08
inner_lr = 0.02
outer_lr = 0.7
nesterov_mu = 0.9
mix_alpha = 0.5
norm_eps = 1e-05

WIRE_SCALE = float(2**18)

ANY = pl.BlockSpec(memory_space=pl.ANY)
VMEM = pl.BlockSpec(memory_space=pltpu.VMEM)
SMEM = pl.BlockSpec(memory_space=pltpu.SMEM)
MIB = 1024 * 1024
CHEAP = pl.CostEstimate(flops=1, bytes_accessed=1, transcendentals=0)


def fsdp_id(z, y, c):
    return (z % 2) * 8 + (y % 4) * 2 + c


def permutation(to):
    return [(fsdp_id(z, y, c), fsdp_id(*to(z, y, c))) for z in range(2) for y in range(4) for c in range(2)]


STRAIGHT = permutation(lambda z, y, c: (z, y + 1 - 2 * c, c))
CROSSED = permutation(lambda z, y, c: (z, y + 2 * c - 1, 1 - c))
OTHER_Z = permutation(lambda z, y, c: (z + 1, y, c))
SIBLING = permutation(lambda z, y, c: (z, y, 1 - c))


def replica_pairs(first):
    pairs = []
    for r in range(8):
        for i in range(16):
            beside = (r % 4) ^ 1 if (i % 2 == 0) == first else 3 - r % 4
            pairs.append((r * 16 + i, (r // 4 * 4 + beside) * 16 + i))
    return pairs


HALF_PAIR = replica_pairs(True)
QUARTER_PAIR = replica_pairs(False)
OPPOSITE = [(r, r // 4 * 4 + (r + 2) % 4) for r in range(8)]
OTHER_H = [(r, (r + 4) % 8) for r in range(8)]


def norm_kernel(x_ref, c_ref, g_ref, u_ref, x_s, g_s, sems):
    g_in = pltpu.make_async_copy(g_ref, g_s, sems.at[0])
    x_in = pltpu.make_async_copy(x_ref, x_s, sems.at[1])
    c_in = pltpu.make_async_copy(c_ref, u_ref.at[1], sems.at[2])
    for copy in (g_in, x_in, c_in):
        copy.start()
    g_in.wait()
    gain = g_s[...].astype(jnp.float32).reshape(1, -1)
    x_in.wait()
    x = x_s[...].astype(jnp.float32)
    scale = lax.rsqrt(jnp.mean(x * x, axis=1, keepdims=True) + norm_eps)
    u_ref[0] = (x * scale * gain).astype(jnp.bfloat16)
    c_in.wait()


def normed_and_cotangent(x, c, gain):
    return pl.pallas_call(
        norm_kernel,
        out_shape=jax.ShapeDtypeStruct((2, *x.shape), jnp.bfloat16),
        in_specs=[ANY, ANY, ANY],
        out_specs=VMEM,
        scratch_shapes=[
            pltpu.VMEM(x.shape, jnp.bfloat16),
            pltpu.VMEM(gain.shape, jnp.bfloat16),
            pltpu.SemaphoreType.DMA((3,)),
        ],
        compiler_params=pltpu.CompilerParams(vmem_limit_bytes=60 * MIB),
        cost_estimate=CHEAP,
        name="norm",
    )(x, c, gain)


class Loads:
    def __init__(self, frag, sems, ahead):
        self.frag, self.sems, self.ahead = frag, sems, ahead
        self.entries, self.started, self.waited = [], 0, 0

    def add(self, name, source, target, without=None):
        copy = pltpu.make_async_copy(source, target, self.sems.at[len(self.entries)])
        self.entries.append((name, copy, without))

    def unless(self, without, act):
        if without is None:
            act()
        else:
            pl.when(self.frag != without)(act)

    def start(self):
        while self.started < min(self.waited + self.ahead, len(self.entries)):
            _, copy, without = self.entries[self.started]
            self.unless(without, copy.start)
            self.started += 1

    def wait(self, name):
        while self.waited < len(self.entries) and self.entries[self.waited][0] == name:
            _, copy, without = self.entries[self.waited]
            self.unless(without, copy.wait)
            self.waited += 1
            self.start()


def right_side(frag, loads, tag, n_s, c_s, w_s, up_s, dh_s, right):
    def dot(left, i):
        return jnp.dot(left[...], w_s[i], preferred_element_type=jnp.float32)

    loads.wait(("n", tag))
    loads.wait(("gate", tag))
    gate = dot(n_s, 0)
    loads.wait(("up", tag))

    @pl.when(frag != 1)
    def _():
        up_s[...] = dot(n_s, 1)

    loads.wait(("c", tag))
    loads.wait(("down", tag))

    @pl.when(frag != 2)
    def _():
        dh_s[...] = dot(c_s, 2)

    sig = jax.nn.sigmoid(gate)

    @pl.when(frag == 0)
    def _():
        right[...] = (dh_s[...] * up_s[...] * sig * (1.0 + gate * (1.0 - sig))).astype(jnp.bfloat16)

    @pl.when(frag == 1)
    def _():
        right[...] = (dh_s[...] * (gate * sig)).astype(jnp.bfloat16)

    @pl.when(frag == 2)
    def _():
        right[...] = (gate * sig * up_s[...]).astype(jnp.bfloat16)


def forward_kernel(count, frag_ref, *refs):
    blocks, weights, out_ref = refs[:count], refs[count : count + 2], refs[count + 2]
    n_s, c_s, w_s, up_s, dh_s, sems = refs[count + 3 :]
    rows, cols = blocks[0].shape[1], weights[0].shape[2]
    frag = frag_ref[0]
    loads = Loads(frag, sems, count + 4)
    for h, weight in enumerate(weights):
        if h == 0:
            for k, b in enumerate(blocks):
                loads.add(("n", h), b.at[0], n_s.at[pl.ds(k * rows, rows)])
        loads.add(("gate", h), weight.at[0], w_s.at[h, 0])
        loads.add(("up", h), weight.at[1], w_s.at[h, 1], 1)
        if h == 0:
            for k, b in enumerate(blocks):
                loads.add(("c", h), b.at[1], c_s.at[pl.ds(k * rows, rows)], 2)
        loads.add(("down", h), weight.at[2], w_s.at[h, 2], 2)
    loads.start()
    for h in range(2):
        right = out_ref.at[:, h * cols : (h + 1) * cols]
        right_side(frag, loads, h, n_s, c_s, w_s.at[h], up_s, dh_s, right)


def forward(frag, blocks, weights):
    count, rows = len(blocks), len(blocks) * blocks[0].shape[1]
    _, d, cols = weights[0].shape
    return pl.pallas_call(
        functools.partial(forward_kernel, count),
        out_shape=jax.ShapeDtypeStruct((rows, 2 * cols), jnp.bfloat16),
        in_specs=[SMEM] + [ANY] * (count + 2),
        out_specs=VMEM,
        scratch_shapes=[
            pltpu.VMEM((rows, d), jnp.bfloat16),
            pltpu.VMEM((rows, d), jnp.bfloat16),
            pltpu.VMEM((2, 3, d, cols), jnp.bfloat16),
            pltpu.VMEM((rows, cols), jnp.float32),
            pltpu.VMEM((rows, cols), jnp.float32),
            pltpu.SemaphoreType.DMA((2 * count + 6,)),
        ],
        compiler_params=pltpu.CompilerParams(vmem_limit_bytes=60 * MIB),
        cost_estimate=CHEAP,
        name="forward",
    )(frag, *blocks, *weights)


def add_gradient(right_t, left, out, total=None):
    step = 768
    for at in range(0, out.shape[1], step):
        span = slice(at, at + step)
        term = jnp.dot(right_t, left[:, span], preferred_element_type=jnp.float32)
        if total is not None:
            term = total[:, span] + term
        out[:, span] = term.astype(out.dtype)


def gradient_kernel(past, spans, frag_ref, block, *refs):
    old_blocks, rights, refs = refs[:past], refs[past : past + len(spans)], refs[past + len(spans) :]
    weights, held, outs = refs[:2], refs[2:4], refs[4:6]
    n_s, c_s, up_s, dh_s, left_s, right_s, sems = refs[6:]
    rows, cols = block.shape[1], weights[0].shape[2]
    frag = frag_ref[0]
    side = jnp.where(frag == 2, 1, 0)
    loads = Loads(frag, sems, 8)
    for h in range(2):
        if h == 0:
            loads.add(("n", h), block.at[0], n_s)
        loads.add(("gate", h), weights[h].at[0], held[h].at[0])
        loads.add(("up", h), weights[h].at[1], held[h].at[1], 1)
        if h == 0:
            loads.add(("c", h), block.at[1], c_s)
        loads.add(("down", h), weights[h].at[2], held[h].at[2], 2)
        if h == 0:
            for right, (at, size) in zip(rights, spans):
                loads.add("rest", right, right_s.at[pl.ds(at, size)])
            for k, b in enumerate((*old_blocks, block)):
                loads.add("rest", b.at[side], left_s.at[pl.ds(k * rows, rows)])
    loads.start()
    for h in range(2):
        here = slice(h * cols, (h + 1) * cols)
        right_side(frag, loads, h, n_s, c_s, held[h], up_s, dh_s, right_s.at[past * rows :, here])
        loads.wait("rest")
        add_gradient(right_s[:, here].T, left_s, outs[h])


def gradients(frag, block, weights, old_blocks, rights):
    past, rows = len(old_blocks), block.shape[1]
    _, d, cols = weights[0].shape
    spans, at = [], 0
    for right in rights:
        spans.append((at, right.shape[0]))
        at += right.shape[0]
    total = at + rows
    out = pl.pallas_call(
        functools.partial(gradient_kernel, past, tuple(spans)),
        out_shape=[jax.ShapeDtypeStruct((3, d, cols), jnp.bfloat16)] * 2 + [jax.ShapeDtypeStruct((cols, d), jnp.float32)] * 2,
        in_specs=[SMEM] + [ANY] * (past + len(spans) + 3),
        out_specs=[VMEM] * 4,
        scratch_shapes=[
            pltpu.VMEM((rows, d), jnp.bfloat16),
            pltpu.VMEM((rows, d), jnp.bfloat16),
            pltpu.VMEM((rows, cols), jnp.float32),
            pltpu.VMEM((rows, cols), jnp.float32),
            pltpu.VMEM((total, d), jnp.bfloat16),
            pltpu.VMEM((total, 2 * cols), jnp.bfloat16),
            pltpu.SemaphoreType.DMA((past + len(spans) + 9,)),
        ],
        compiler_params=pltpu.CompilerParams(vmem_limit_bytes=20 * MIB),
        cost_estimate=CHEAP,
        name="gradients",
    )(frag, block, *old_blocks, *rights, *weights)
    return out[:2], out[2:]


def step_kernel(count, frag_ref, *refs):
    blocks, (weight, total, out) = refs[:count], refs[count : count + 3]
    n_s, c_s, up_s, dh_s, right_s, sems = refs[count + 3 :]
    rows = blocks[0].shape[1]
    frag = frag_ref[0]
    loads = Loads(frag, sems, 2 * count)
    for kind, side, target in (("n", 0, n_s), ("c", 1, c_s)):
        for k, block in enumerate(blocks):
            loads.add((kind, 0), block.at[side], target.at[pl.ds(k * rows, rows)])
    loads.start()
    right_side(frag, loads, 0, n_s, c_s, weight, up_s, dh_s, right_s)
    right_t = right_s[...].T
    pl.when(frag == 2)(functools.partial(add_gradient, right_t, c_s, out, total))
    pl.when(frag != 2)(functools.partial(add_gradient, right_t, n_s, out, total))


def add_blocks(frag, blocks, weight, total, kind=jnp.float32):
    count, rows = len(blocks), len(blocks) * blocks[0].shape[1]
    _, d, cols = weight.shape
    return pl.pallas_call(
        functools.partial(step_kernel, count),
        out_shape=jax.ShapeDtypeStruct((cols, d), kind),
        in_specs=[SMEM] + [ANY] * count + [VMEM] * 2,
        out_specs=VMEM,
        scratch_shapes=[
            pltpu.VMEM((rows, d), jnp.bfloat16),
            pltpu.VMEM((rows, d), jnp.bfloat16),
            pltpu.VMEM((rows, cols), jnp.float32),
            pltpu.VMEM((rows, cols), jnp.float32),
            pltpu.VMEM((rows, cols), jnp.bfloat16),
            pltpu.SemaphoreType.DMA((2 * count,)),
        ],
        input_output_aliases={count + 2: 0} if kind == jnp.float32 else {},
        compiler_params=pltpu.CompilerParams(vmem_limit_bytes=12 * MIB),
        cost_estimate=CHEAP,
        name="blocks",
    )(frag, *blocks, weight, total)


def adam_kernel(tokens, tile, own_ref, other_ref, m_ref, v_ref, mixed_ref, out_ref, out_s, sems):
    copies = []
    for i in range(m_ref.shape[0] // tile):
        span = slice(i * tile, (i + 1) * tile)
        grad = (own_ref[:, span] + other_ref[:, span].astype(jnp.float32)).T * (1.0 / tokens)
        moment_one = beta_one * m_ref[span, :] + (1.0 - beta_one) * grad
        moment_two = beta_two * v_ref[span, :] + (1.0 - beta_two) * grad * grad
        step_inner = inner_lr * moment_one / (jnp.sqrt(moment_two) + adam_eps)
        out_s[span, :] = (mixed_ref[span, :] - mix_alpha * step_inner).astype(jnp.bfloat16)
        copy = pltpu.make_async_copy(out_s.at[span, :], out_ref.at[span, :], sems.at[i])
        copy.start()
        copies.append(copy)
    for copy in copies:
        copy.wait()


def adam(tokens, own, other, m, v, mixed):
    d, cols = m.shape
    tile = 512
    return pl.pallas_call(
        functools.partial(adam_kernel, tokens, tile),
        out_shape=jax.ShapeDtypeStruct((d, cols), jnp.bfloat16),
        in_specs=[VMEM] * 5,
        out_specs=ANY,
        scratch_shapes=[pltpu.VMEM((d, cols), jnp.bfloat16), pltpu.SemaphoreType.DMA((d // tile,))],
        compiler_params=pltpu.CompilerParams(vmem_limit_bytes=12 * MIB),
        cost_estimate=CHEAP,
        name="adam",
    )(own, other, m, v, mixed)


def after(value, *others):
    return lax.optimization_barrier((value, *others))[0]


def per_device(step, hidden_in, cotangent, norm_gain, weights, adam_m, adam_v, global_frag, outer_mom):
    fragment = step[0] % 3
    frag = fragment.reshape(1)
    w_own = weights[0]
    w_sib = lax.ppermute(w_own, "fsdp", SIBLING)
    w_both = [w_sib, w_own]
    own = normed_and_cotangent(hidden_in[0], cotangent[0], norm_gain)

    straight = functools.partial(lax.ppermute, axis_name="fsdp", perm=STRAIGHT)
    crossed = functools.partial(lax.ppermute, axis_name="fsdp", perm=CROSSED)
    other_z = functools.partial(lax.ppermute, axis_name="fsdp", perm=OTHER_Z)

    x = lax.rem(lax.axis_index("replica"), 4)
    first_core = lax.rem(lax.axis_index("fsdp"), 2) == 0
    inner, upper = lax.rem((x + 1) // 2, 2), x // 2
    h = jnp.where(first_core, inner, upper)
    q = jnp.where(first_core, upper, inner)
    everyone = ("replica", "fsdp")
    d, cols = global_frag.shape
    half, quarter = d // 2, d // 4

    def w_rows(at, size):
        return lax.dynamic_slice(w_own, (fragment, at, 0), (1, size, cols))[0]

    def g_rows(at, size):
        return lax.dynamic_slice(global_frag, (at, 0), (size, cols))

    def ordered(second, first, other):
        return jnp.where(second == 0, jnp.concatenate([first, other]), jnp.concatenate([other, first]))

    def wire(value):
        return (value * (WIRE_SCALE / 8)).astype(jnp.float16)

    near = straight(own)
    z_own = other_z(own)
    cross = crossed(own)
    w_pair = lax.ppermute(after(w_rows((1 - h) * half, half), own), everyone, HALF_PAIR)

    def pair_delta(at):
        base = g_rows(h * half + at, quarter)
        mine = w_rows(h * half + at, quarter).astype(jnp.float32)
        theirs = lax.dynamic_slice_in_dim(w_pair, at, quarter).astype(jnp.float32)
        return (base - mine) + (base - theirs)

    sent = wire(pair_delta((1 - q) * quarter))
    got = lax.ppermute(sent, everyone, QUARTER_PAIR)
    part = wire(pair_delta(q * quarter) + got.astype(jnp.float32) * (8 / WIRE_SCALE))
    z_own, near, part = lax.optimization_barrier((z_own, near, part))
    other = lax.ppermute(part, "replica", OTHER_H)
    z_near = straight(z_own)
    far = straight(near)
    first = [own, near, cross, z_own]
    right = forward(frag, first, w_both)
    other = after(other, right)
    mine = (part.astype(jnp.float32) + other.astype(jnp.float32)).astype(jnp.float16)
    cross, mine = lax.optimization_barrier((cross, mine))
    z_cross = other_z(cross)
    beside, across = lax.ppermute(mine, everyone, QUARTER_PAIR), lax.ppermute(mine, everyone, HALF_PAIR)
    opposite = lax.ppermute(mine, "replica", OPPOSITE)
    rights = [right, forward(frag, [z_near], w_both)]
    z_far = straight(after(z_near, beside, rights[1]))

    delta = ordered(h, ordered(q, mine, beside), ordered(q, across, opposite)).astype(jnp.float32) * (1 / WIRE_SCALE)
    momentum_new = nesterov_mu * outer_mom + delta
    global_new = global_frag - outer_lr * (delta + nesterov_mu * momentum_new)
    mixed = mix_alpha * w_rows(0, d).astype(jnp.float32) + (1.0 - mix_alpha) * global_new

    held, totals = gradients(frag, after(far, mixed), w_both, [*first, z_near], rights)
    sib_total = add_blocks(frag, [z_cross], held[0], totals[0])
    grad_sib = add_blocks(frag, [z_far], held[0], sib_total, jnp.bfloat16)
    grad_sib = lax.ppermute(grad_sib, "fsdp", SIBLING)
    grad_own = add_blocks(frag, [z_cross, z_far], held[1], totals[1])
    tokens_total = hidden_in.shape[1] * lax.axis_size("fsdp")
    merged = adam(tokens_total, grad_own, grad_sib, adam_m[0], adam_v[0], mixed)
    return (global_new, momentum_new, merged[None])


def solution(mesh):
    placed = (
        P(),
        P("replica", "fsdp", None),
        P("replica", "fsdp", None),
        P(),
        P("replica", None, None, "fsdp"),
        P("replica", None, "fsdp"),
        P("replica", None, "fsdp"),
        P(None, "fsdp"),
        P(None, "fsdp"),
    )
    return jax.shard_map(
        per_device,
        mesh=mesh,
        in_specs=placed,
        out_specs=(P(None, "fsdp"), P(None, "fsdp"), P("replica", None, "fsdp")),
        check_vma=False,
    )
```

```python
import functools

import jax
import jax.numpy as jnp
from jax import lax
from jax.experimental import pallas as pl
from jax.experimental.pallas import tpu as pltpu
from jax.sharding import PartitionSpec as P

beta_one = 0.9
beta_two = 0.95
adam_eps = 1e-08
inner_lr = 0.02
outer_lr = 0.7
nesterov_mu = 0.9
mix_alpha = 0.5
norm_eps = 1e-05

WIRE_SCALE = float(2**18)

ANY = pl.BlockSpec(memory_space=pl.ANY)
VMEM = pl.BlockSpec(memory_space=pltpu.VMEM)
SMEM = pl.BlockSpec(memory_space=pltpu.SMEM)
MIB = 1024 * 1024
CHEAP = pl.CostEstimate(flops=1, bytes_accessed=1, transcendentals=0)


def fsdp_id(z, y, c):
    return (z % 2) * 8 + (y % 4) * 2 + c


def permutation(to):
    return [(fsdp_id(z, y, c), fsdp_id(*to(z, y, c))) for z in range(2) for y in range(4) for c in range(2)]


STRAIGHT = permutation(lambda z, y, c: (z, y + 1 - 2 * c, c))
CROSSED = permutation(lambda z, y, c: (z, y + 2 * c - 1, 1 - c))
OTHER_Z = permutation(lambda z, y, c: (z + 1, y, c))
SIBLING = permutation(lambda z, y, c: (z, y, 1 - c))


def replica_pairs(first):
    pairs = []
    for r in range(8):
        for i in range(16):
            beside = (r % 4) ^ 1 if (i % 2 == 0) == first else 3 - r % 4
            pairs.append((r * 16 + i, (r // 4 * 4 + beside) * 16 + i))
    return pairs


HALF_PAIR = replica_pairs(True)
QUARTER_PAIR = replica_pairs(False)
OPPOSITE = [(r, r // 4 * 4 + (r + 2) % 4) for r in range(8)]
OTHER_H = [(r, (r + 4) % 8) for r in range(8)]


def norm_kernel(x_ref, c_ref, g_ref, u_ref, x_s, g_s, sems):
    g_in = pltpu.make_async_copy(g_ref, g_s, sems.at[0])
    c_in = pltpu.make_async_copy(c_ref, u_ref.at[1], sems.at[1])
    tile = x_ref.shape[0] // 2
    spans = [pl.ds(0, tile), pl.ds(tile, tile)]
    x_in = [pltpu.make_async_copy(x_ref.at[span], x_s.at[span], sems.at[2 + i]) for i, span in enumerate(spans)]
    for copy in (g_in, *x_in, c_in):
        copy.start()
    g_in.wait()
    gain = g_s[...].astype(jnp.float32).reshape(1, -1)
    for span, copy in zip(spans, x_in):
        copy.wait()
        x = x_s[span].astype(jnp.float32)
        scale = lax.rsqrt(jnp.mean(x * x, axis=1, keepdims=True) + norm_eps)
        u_ref[0, span] = (x * scale * gain).astype(jnp.bfloat16)
    c_in.wait()


def normed_and_cotangent(x, c, gain):
    return pl.pallas_call(
        norm_kernel,
        out_shape=jax.ShapeDtypeStruct((2, *x.shape), jnp.bfloat16),
        in_specs=[ANY, ANY, ANY],
        out_specs=VMEM,
        scratch_shapes=[
            pltpu.VMEM(x.shape, jnp.bfloat16),
            pltpu.VMEM(gain.shape, jnp.bfloat16),
            pltpu.SemaphoreType.DMA((4,)),
        ],
        compiler_params=pltpu.CompilerParams(vmem_limit_bytes=60 * MIB),
        cost_estimate=CHEAP,
        name="norm",
    )(x, c, gain)


class Loads:
    def __init__(self, frag, sems, ahead):
        self.frag, self.sems, self.ahead = frag, sems, ahead
        self.entries, self.started, self.waited = [], 0, 0

    def add(self, name, source, target, without=None):
        copy = pltpu.make_async_copy(source, target, self.sems.at[len(self.entries)])
        self.entries.append((name, copy, without))

    def unless(self, without, act):
        if without is None:
            act()
        else:
            pl.when(self.frag != without)(act)

    def start(self):
        while self.started < min(self.waited + self.ahead, len(self.entries)):
            _, copy, without = self.entries[self.started]
            self.unless(without, copy.start)
            self.started += 1

    def wait(self, name):
        while self.waited < len(self.entries) and self.entries[self.waited][0] == name:
            _, copy, without = self.entries[self.waited]
            self.unless(without, copy.wait)
            self.waited += 1
            self.start()


def right_side(frag, loads, tag, n_s, c_s, w_s, up_s, dh_s, right):
    def dot(left, i):
        return jnp.dot(left[...], w_s[i], preferred_element_type=jnp.float32)

    loads.wait(("n", tag))
    loads.wait(("gate", tag))
    gate = dot(n_s, 0)
    loads.wait(("up", tag))

    @pl.when(frag != 1)
    def _():
        up_s[...] = dot(n_s, 1)

    loads.wait(("c", tag))
    loads.wait(("down", tag))

    @pl.when(frag != 2)
    def _():
        dh_s[...] = dot(c_s, 2)

    sig = jax.nn.sigmoid(gate)

    @pl.when(frag == 0)
    def _():
        right[...] = (dh_s[...] * up_s[...] * sig * (1.0 + gate * (1.0 - sig))).astype(jnp.bfloat16)

    @pl.when(frag == 1)
    def _():
        right[...] = (dh_s[...] * (gate * sig)).astype(jnp.bfloat16)

    @pl.when(frag == 2)
    def _():
        right[...] = (gate * sig * up_s[...]).astype(jnp.bfloat16)


def forward_kernel(count, frag_ref, *refs):
    blocks, weights, out_ref = refs[:count], refs[count : count + 2], refs[count + 2]
    n_s, c_s, w_s, up_s, dh_s, sems = refs[count + 3 :]
    rows, cols = blocks[0].shape[1], weights[0].shape[2]
    frag = frag_ref[0]
    loads = Loads(frag, sems, count + 4)
    for h, weight in enumerate(weights):
        if h == 0:
            for k, b in enumerate(blocks):
                loads.add(("n", h), b.at[0], n_s.at[pl.ds(k * rows, rows)])
        loads.add(("gate", h), weight.at[0], w_s.at[h, 0])
        loads.add(("up", h), weight.at[1], w_s.at[h, 1], 1)
        if h == 0:
            for k, b in enumerate(blocks):
                loads.add(("c", h), b.at[1], c_s.at[pl.ds(k * rows, rows)], 2)
        loads.add(("down", h), weight.at[2], w_s.at[h, 2], 2)
    loads.start()
    for h in range(2):
        right = out_ref.at[:, h * cols : (h + 1) * cols]
        right_side(frag, loads, h, n_s, c_s, w_s.at[h], up_s, dh_s, right)


def forward(frag, blocks, weights):
    count, rows = len(blocks), len(blocks) * blocks[0].shape[1]
    _, d, cols = weights[0].shape
    return pl.pallas_call(
        functools.partial(forward_kernel, count),
        out_shape=jax.ShapeDtypeStruct((rows, 2 * cols), jnp.bfloat16),
        in_specs=[SMEM] + [ANY] * (count + 2),
        out_specs=VMEM,
        scratch_shapes=[
            pltpu.VMEM((rows, d), jnp.bfloat16),
            pltpu.VMEM((rows, d), jnp.bfloat16),
            pltpu.VMEM((2, 3, d, cols), jnp.bfloat16),
            pltpu.VMEM((rows, cols), jnp.float32),
            pltpu.VMEM((rows, cols), jnp.float32),
            pltpu.SemaphoreType.DMA((2 * count + 6,)),
        ],
        compiler_params=pltpu.CompilerParams(vmem_limit_bytes=60 * MIB),
        cost_estimate=CHEAP,
        name="forward",
    )(frag, *blocks, *weights)


def add_gradient(right_t, left, out, total=None):
    step = 768
    for at in range(0, out.shape[1], step):
        span = slice(at, at + step)
        term = jnp.dot(right_t, left[:, span], preferred_element_type=jnp.float32)
        if total is not None:
            term = total[:, span] + term
        out[:, span] = term.astype(out.dtype)


def gradient_kernel(past, spans, frag_ref, block, *refs):
    old_blocks, rights, refs = refs[:past], refs[past : past + len(spans)], refs[past + len(spans) :]
    weights, held, outs = refs[:2], refs[2:4], refs[4:6]
    n_s, c_s, up_s, dh_s, left_s, right_s, sems = refs[6:]
    rows, cols = block.shape[1], weights[0].shape[2]
    frag = frag_ref[0]
    side = jnp.where(frag == 2, 1, 0)
    loads = Loads(frag, sems, 8)
    for h in range(2):
        if h == 0:
            loads.add(("n", h), block.at[0], n_s)
        loads.add(("gate", h), weights[h].at[0], held[h].at[0])
        loads.add(("up", h), weights[h].at[1], held[h].at[1], 1)
        if h == 0:
            loads.add(("c", h), block.at[1], c_s)
        loads.add(("down", h), weights[h].at[2], held[h].at[2], 2)
        if h == 0:
            for right, (at, size) in zip(rights, spans):
                loads.add("rest", right, right_s.at[pl.ds(at, size)])
            for k, b in enumerate((*old_blocks, block)):
                loads.add("rest", b.at[side], left_s.at[pl.ds(k * rows, rows)])
    loads.start()
    for h in range(2):
        here = slice(h * cols, (h + 1) * cols)
        right_side(frag, loads, h, n_s, c_s, held[h], up_s, dh_s, right_s.at[past * rows :, here])
        loads.wait("rest")
        add_gradient(right_s[:, here].T, left_s, outs[h])


def gradients(frag, block, weights, old_blocks, rights):
    past, rows = len(old_blocks), block.shape[1]
    _, d, cols = weights[0].shape
    spans, at = [], 0
    for right in rights:
        spans.append((at, right.shape[0]))
        at += right.shape[0]
    total = at + rows
    out = pl.pallas_call(
        functools.partial(gradient_kernel, past, tuple(spans)),
        out_shape=[jax.ShapeDtypeStruct((3, d, cols), jnp.bfloat16)] * 2 + [jax.ShapeDtypeStruct((cols, d), jnp.float32)] * 2,
        in_specs=[SMEM] + [ANY] * (past + len(spans) + 3),
        out_specs=[VMEM] * 4,
        scratch_shapes=[
            pltpu.VMEM((rows, d), jnp.bfloat16),
            pltpu.VMEM((rows, d), jnp.bfloat16),
            pltpu.VMEM((rows, cols), jnp.float32),
            pltpu.VMEM((rows, cols), jnp.float32),
            pltpu.VMEM((total, d), jnp.bfloat16),
            pltpu.VMEM((total, 2 * cols), jnp.bfloat16),
            pltpu.SemaphoreType.DMA((past + len(spans) + 9,)),
        ],
        compiler_params=pltpu.CompilerParams(vmem_limit_bytes=20 * MIB),
        cost_estimate=CHEAP,
        name="gradients",
    )(frag, block, *old_blocks, *rights, *weights)
    return out[:2], out[2:]


def step_kernel(count, frag_ref, *refs):
    blocks, (weight, total, out) = refs[:count], refs[count : count + 3]
    n_s, c_s, up_s, dh_s, right_s, sems = refs[count + 3 :]
    rows = blocks[0].shape[1]
    frag = frag_ref[0]
    loads = Loads(frag, sems, 2 * count)
    for kind, side, target in (("n", 0, n_s), ("c", 1, c_s)):
        for k, block in enumerate(blocks):
            loads.add((kind, 0), block.at[side], target.at[pl.ds(k * rows, rows)])
    loads.start()
    right_side(frag, loads, 0, n_s, c_s, weight, up_s, dh_s, right_s)
    right_t = right_s[...].T
    pl.when(frag == 2)(functools.partial(add_gradient, right_t, c_s, out, total))
    pl.when(frag != 2)(functools.partial(add_gradient, right_t, n_s, out, total))


def add_blocks(frag, blocks, weight, total, kind=jnp.float32, cost=CHEAP):
    count, rows = len(blocks), len(blocks) * blocks[0].shape[1]
    _, d, cols = weight.shape
    return pl.pallas_call(
        functools.partial(step_kernel, count),
        out_shape=jax.ShapeDtypeStruct((cols, d), kind),
        in_specs=[SMEM] + [ANY] * count + [VMEM] * 2,
        out_specs=VMEM,
        scratch_shapes=[
            pltpu.VMEM((rows, d), jnp.bfloat16),
            pltpu.VMEM((rows, d), jnp.bfloat16),
            pltpu.VMEM((rows, cols), jnp.float32),
            pltpu.VMEM((rows, cols), jnp.float32),
            pltpu.VMEM((rows, cols), jnp.bfloat16),
            pltpu.SemaphoreType.DMA((2 * count,)),
        ],
        input_output_aliases={count + 2: 0} if kind == jnp.float32 else {},
        compiler_params=pltpu.CompilerParams(vmem_limit_bytes=12 * MIB),
        cost_estimate=cost,
        name="blocks",
    )(frag, *blocks, weight, total)


def adam_kernel(tokens, tile, own_ref, other_ref, m_ref, v_ref, mixed_ref, out_ref, out_s, sems):
    copies = []
    for i in range(m_ref.shape[0] // tile):
        span = slice(i * tile, (i + 1) * tile)
        grad = (own_ref[:, span] + other_ref[:, span].astype(jnp.float32)).T * (1.0 / tokens)
        moment_one = beta_one * m_ref[span, :] + (1.0 - beta_one) * grad
        moment_two = beta_two * v_ref[span, :] + (1.0 - beta_two) * grad * grad
        root = moment_two * lax.rsqrt(moment_two)
        step_inner = inner_lr * moment_one / (root + adam_eps)
        out_s[span, :] = (mixed_ref[span, :] - mix_alpha * step_inner).astype(jnp.bfloat16)
        copy = pltpu.make_async_copy(out_s.at[span, :], out_ref.at[span, :], sems.at[i])
        copy.start()
        copies.append(copy)
    for copy in copies:
        copy.wait()


def adam(tokens, own, other, m, v, mixed):
    d, cols = m.shape
    tile = 512
    return pl.pallas_call(
        functools.partial(adam_kernel, tokens, tile),
        out_shape=jax.ShapeDtypeStruct((d, cols), jnp.bfloat16),
        in_specs=[VMEM] * 5,
        out_specs=ANY,
        scratch_shapes=[pltpu.VMEM((d, cols), jnp.bfloat16), pltpu.SemaphoreType.DMA((d // tile,))],
        compiler_params=pltpu.CompilerParams(vmem_limit_bytes=12 * MIB),
        cost_estimate=CHEAP,
        name="adam",
    )(own, other, m, v, mixed)


def after(value, *others):
    return lax.optimization_barrier((value, *others))[0]


def per_device(step, hidden_in, cotangent, norm_gain, weights, adam_m, adam_v, global_frag, outer_mom):
    fragment = step[0] % 3
    frag = fragment.reshape(1)
    w_own = weights[0]
    w_sib = lax.ppermute(w_own, "fsdp", SIBLING)
    w_both = [w_sib, w_own]
    own = normed_and_cotangent(hidden_in[0], cotangent[0], norm_gain)

    straight = functools.partial(lax.ppermute, axis_name="fsdp", perm=STRAIGHT)
    crossed = functools.partial(lax.ppermute, axis_name="fsdp", perm=CROSSED)
    other_z = functools.partial(lax.ppermute, axis_name="fsdp", perm=OTHER_Z)

    x = lax.rem(lax.axis_index("replica"), 4)
    first_core = lax.rem(lax.axis_index("fsdp"), 2) == 0
    inner, upper = lax.rem((x + 1) // 2, 2), x // 2
    h = jnp.where(first_core, inner, upper)
    q = jnp.where(first_core, upper, inner)
    everyone = ("replica", "fsdp")
    d, cols = global_frag.shape
    half, quarter = d // 2, d // 4

    def w_rows(at, size):
        return lax.dynamic_slice(w_own, (fragment, at, 0), (1, size, cols))[0]

    def g_rows(at, size):
        return lax.dynamic_slice(global_frag, (at, 0), (size, cols))

    def ordered(second, first, other):
        return jnp.where(second == 0, jnp.concatenate([first, other]), jnp.concatenate([other, first]))

    def wire(value):
        return (value * (WIRE_SCALE / 8)).astype(jnp.float16)

    near = straight(own)
    z_own = other_z(own)
    cross = crossed(own)
    w_pair = lax.ppermute(after(w_rows((1 - h) * half, half), own), everyone, HALF_PAIR)

    def pair_delta(at):
        base = g_rows(h * half + at, quarter)
        mine = w_rows(h * half + at, quarter).astype(jnp.float32)
        theirs = lax.dynamic_slice_in_dim(w_pair, at, quarter).astype(jnp.float32)
        return (base - mine) + (base - theirs)

    sent = wire(pair_delta((1 - q) * quarter))
    got = lax.ppermute(sent, everyone, QUARTER_PAIR)
    part = wire(pair_delta(q * quarter) + got.astype(jnp.float32) * (8 / WIRE_SCALE))
    z_own, near, part = lax.optimization_barrier((z_own, near, part))
    other = lax.ppermute(part, "replica", OTHER_H)
    z_near = straight(z_own)
    far = straight(near)
    first = [own, near, cross, z_own]
    right = forward(frag, first, w_both)
    other = after(other, right)
    mine = (part.astype(jnp.float32) + other.astype(jnp.float32)).astype(jnp.float16)
    cross, mine = lax.optimization_barrier((cross, mine))
    z_cross = other_z(cross)
    beside, across = lax.ppermute(mine, everyone, QUARTER_PAIR), lax.ppermute(mine, everyone, HALF_PAIR)
    opposite = lax.ppermute(mine, "replica", OPPOSITE)
    rights = [right, forward(frag, [z_near], w_both)]
    z_far = straight(after(z_near, beside, rights[1]))

    delta = ordered(h, ordered(q, mine, beside), ordered(q, across, opposite)).astype(jnp.float32) * (1 / WIRE_SCALE)
    momentum_new = nesterov_mu * outer_mom + delta
    global_new = global_frag - outer_lr * (delta + nesterov_mu * momentum_new)
    mixed = mix_alpha * w_rows(0, d).astype(jnp.float32) + (1.0 - mix_alpha) * global_new

    held, totals = gradients(frag, after(far, mixed), w_both, [*first, z_near], rights)
    cost = pl.CostEstimate(flops=8 * z_cross.size * cols, bytes_accessed=3 * totals[0].size * 4, transcendentals=0)
    sib_total = add_blocks(frag, [z_cross], held[0], totals[0], cost=cost)
    grad_sib = add_blocks(frag, [z_far], held[0], sib_total, jnp.bfloat16)
    grad_sib = lax.ppermute(grad_sib, "fsdp", SIBLING)
    grad_own = add_blocks(frag, [z_cross, z_far], held[1], totals[1])
    tokens_total = hidden_in.shape[1] * lax.axis_size("fsdp")
    merged = adam(tokens_total, grad_own, grad_sib, adam_m[0], adam_v[0], mixed)
    return (global_new, momentum_new, merged[None])


def solution(mesh):
    placed = (
        P(),
        P("replica", "fsdp", None),
        P("replica", "fsdp", None),
        P(),
        P("replica", None, None, "fsdp"),
        P("replica", None, "fsdp"),
        P("replica", None, "fsdp"),
        P(None, "fsdp"),
        P(None, "fsdp"),
    )
    return jax.shard_map(
        per_device,
        mesh=mesh,
        in_specs=placed,
        out_specs=(P(None, "fsdp"), P(None, "fsdp"), P("replica", None, "fsdp")),
        check_vma=False,
    )
```

```python
import functools

import jax
import jax.numpy as jnp
from jax import lax
from jax.experimental import pallas as pl
from jax.experimental.pallas import tpu as pltpu
from jax.sharding import PartitionSpec as P

beta_one = 0.9
beta_two = 0.95
adam_eps = 1e-08
inner_lr = 0.02
outer_lr = 0.7
nesterov_mu = 0.9
mix_alpha = 0.5
norm_eps = 1e-05

WIRE_SCALE = float(2**18)

ANY = pl.BlockSpec(memory_space=pl.ANY)
VMEM = pl.BlockSpec(memory_space=pltpu.VMEM)
SMEM = pl.BlockSpec(memory_space=pltpu.SMEM)
MIB = 1024 * 1024
CHEAP = pl.CostEstimate(flops=1, bytes_accessed=1, transcendentals=0)


def fsdp_id(z, y, c):
    return (z % 2) * 8 + (y % 4) * 2 + c


def permutation(to):
    return [(fsdp_id(z, y, c), fsdp_id(*to(z, y, c))) for z in range(2) for y in range(4) for c in range(2)]


STRAIGHT = permutation(lambda z, y, c: (z, y + 1 - 2 * c, c))
CROSSED = permutation(lambda z, y, c: (z, y + 2 * c - 1, 1 - c))
OTHER_Z = permutation(lambda z, y, c: (z + 1, y, c))
SIBLING = permutation(lambda z, y, c: (z, y, 1 - c))


def replica_pairs(first):
    pairs = []
    for r in range(8):
        for i in range(16):
            beside = (r % 4) ^ 1 if (i % 2 == 0) == first else 3 - r % 4
            pairs.append((r * 16 + i, (r // 4 * 4 + beside) * 16 + i))
    return pairs


HALF_PAIR = replica_pairs(True)
QUARTER_PAIR = replica_pairs(False)
OPPOSITE = [(r, r // 4 * 4 + (r + 2) % 4) for r in range(8)]
OTHER_H = [(r, (r + 4) % 8) for r in range(8)]


def norm_kernel(x_ref, c_ref, g_ref, u_ref, x_s, g_s, sems):
    g_in = pltpu.make_async_copy(g_ref, g_s, sems.at[0])
    c_in = pltpu.make_async_copy(c_ref, u_ref.at[1], sems.at[1])
    tile = x_ref.shape[0] // 2
    spans = [pl.ds(0, tile), pl.ds(tile, tile)]
    x_in = [pltpu.make_async_copy(x_ref.at[span], x_s.at[span], sems.at[2 + i]) for i, span in enumerate(spans)]
    for copy in (g_in, *x_in, c_in):
        copy.start()
    g_in.wait()
    gain = g_s[...].astype(jnp.float32).reshape(1, -1)
    for span, copy in zip(spans, x_in):
        copy.wait()
        x = x_s[span].astype(jnp.float32)
        scale = lax.rsqrt(jnp.mean(x * x, axis=1, keepdims=True) + norm_eps)
        u_ref[0, span] = (x * scale * gain).astype(jnp.bfloat16)
    c_in.wait()


def normed_and_cotangent(x, c, gain):
    return pl.pallas_call(
        norm_kernel,
        out_shape=jax.ShapeDtypeStruct((2, *x.shape), jnp.bfloat16),
        in_specs=[ANY, ANY, ANY],
        out_specs=VMEM,
        scratch_shapes=[
            pltpu.VMEM(x.shape, jnp.bfloat16),
            pltpu.VMEM(gain.shape, jnp.bfloat16),
            pltpu.SemaphoreType.DMA((4,)),
        ],
        compiler_params=pltpu.CompilerParams(vmem_limit_bytes=60 * MIB),
        cost_estimate=CHEAP,
        name="norm",
    )(x, c, gain)


class Loads:
    def __init__(self, frag, sems, ahead):
        self.frag, self.sems, self.ahead = frag, sems, ahead
        self.entries, self.started, self.waited = [], 0, 0

    def add(self, name, source, target, without=None):
        copy = pltpu.make_async_copy(source, target, self.sems.at[len(self.entries)])
        self.entries.append((name, copy, without))

    def unless(self, without, act):
        if without is None:
            act()
        else:
            pl.when(self.frag != without)(act)

    def start(self):
        while self.started < min(self.waited + self.ahead, len(self.entries)):
            _, copy, without = self.entries[self.started]
            self.unless(without, copy.start)
            self.started += 1

    def wait(self, name):
        while self.waited < len(self.entries) and self.entries[self.waited][0] == name:
            _, copy, without = self.entries[self.waited]
            self.unless(without, copy.wait)
            self.waited += 1
            self.start()


def right_side(frag, loads, tag, n_s, c_s, w_s, up_s, dh_s, right):
    def dot(left, i):
        return jnp.dot(left[...], w_s[i], preferred_element_type=jnp.float32)

    loads.wait(("n", tag))
    loads.wait(("gate", tag))
    gate = dot(n_s, 0)
    loads.wait(("up", tag))

    @pl.when(frag != 1)
    def _():
        up_s[...] = dot(n_s, 1)

    loads.wait(("c", tag))
    loads.wait(("down", tag))

    @pl.when(frag != 2)
    def _():
        dh_s[...] = dot(c_s, 2)

    sig = jax.nn.sigmoid(gate)

    @pl.when(frag == 0)
    def _():
        right[...] = (dh_s[...] * up_s[...] * sig * (1.0 + gate * (1.0 - sig))).astype(jnp.bfloat16)

    @pl.when(frag == 1)
    def _():
        right[...] = (dh_s[...] * (gate * sig)).astype(jnp.bfloat16)

    @pl.when(frag == 2)
    def _():
        right[...] = (gate * sig * up_s[...]).astype(jnp.bfloat16)


def forward_kernel(count, frag_ref, *refs):
    blocks, weights, out_ref = refs[:count], refs[count : count + 2], refs[count + 2]
    n_s, c_s, w_s, up_s, dh_s, sems = refs[count + 3 :]
    rows, cols = blocks[0].shape[1], weights[0].shape[2]
    frag = frag_ref[0]
    loads = Loads(frag, sems, count + 4)
    for h, weight in enumerate(weights):
        if h == 0:
            for k, b in enumerate(blocks):
                loads.add(("n", h), b.at[0], n_s.at[pl.ds(k * rows, rows)])
        loads.add(("gate", h), weight.at[0], w_s.at[h, 0])
        loads.add(("up", h), weight.at[1], w_s.at[h, 1], 1)
        if h == 0:
            for k, b in enumerate(blocks):
                loads.add(("c", h), b.at[1], c_s.at[pl.ds(k * rows, rows)], 2)
        loads.add(("down", h), weight.at[2], w_s.at[h, 2], 2)
    loads.start()
    for h in range(2):
        right = out_ref.at[:, h * cols : (h + 1) * cols]
        right_side(frag, loads, h, n_s, c_s, w_s.at[h], up_s, dh_s, right)


def forward(frag, blocks, weights):
    count, rows = len(blocks), len(blocks) * blocks[0].shape[1]
    _, d, cols = weights[0].shape
    return pl.pallas_call(
        functools.partial(forward_kernel, count),
        out_shape=jax.ShapeDtypeStruct((rows, 2 * cols), jnp.bfloat16),
        in_specs=[SMEM] + [ANY] * (count + 2),
        out_specs=VMEM,
        scratch_shapes=[
            pltpu.VMEM((rows, d), jnp.bfloat16),
            pltpu.VMEM((rows, d), jnp.bfloat16),
            pltpu.VMEM((2, 3, d, cols), jnp.bfloat16),
            pltpu.VMEM((rows, cols), jnp.float32),
            pltpu.VMEM((rows, cols), jnp.float32),
            pltpu.SemaphoreType.DMA((2 * count + 6,)),
        ],
        compiler_params=pltpu.CompilerParams(vmem_limit_bytes=60 * MIB),
        cost_estimate=CHEAP,
        name="forward",
    )(frag, *blocks, *weights)


def add_gradient(right_t, left, out, total=None):
    step = 768
    for at in range(0, out.shape[1], step):
        span = slice(at, at + step)
        term = jnp.dot(right_t, left[:, span], preferred_element_type=jnp.float32)
        if total is not None:
            term = total[:, span] + term
        out[:, span] = term.astype(out.dtype)


def gradient_kernel(past, spans, frag_ref, block, *refs):
    old_blocks, rights, refs = refs[:past], refs[past : past + len(spans)], refs[past + len(spans) :]
    weights, held, outs = refs[:2], refs[2:4], refs[4:6]
    n_s, c_s, up_s, dh_s, left_s, right_s, sems = refs[6:]
    rows, cols = block.shape[1], weights[0].shape[2]
    frag = frag_ref[0]
    side = jnp.where(frag == 2, 1, 0)
    loads = Loads(frag, sems, 8)
    for h in range(2):
        if h == 0:
            loads.add(("n", h), block.at[0], n_s)
        loads.add(("gate", h), weights[h].at[0], held[h].at[0])
        loads.add(("up", h), weights[h].at[1], held[h].at[1], 1)
        if h == 0:
            loads.add(("c", h), block.at[1], c_s)
        loads.add(("down", h), weights[h].at[2], held[h].at[2], 2)
        if h == 0:
            for right, (at, size) in zip(rights, spans):
                loads.add("rest", right, right_s.at[pl.ds(at, size)])
            for k, b in enumerate((*old_blocks, block)):
                loads.add("rest", b.at[side], left_s.at[pl.ds(k * rows, rows)])
    loads.start()
    for h in range(2):
        here = slice(h * cols, (h + 1) * cols)
        right_side(frag, loads, h, n_s, c_s, held[h], up_s, dh_s, right_s.at[past * rows :, here])
        loads.wait("rest")
        add_gradient(right_s[:, here].T, left_s, outs[h])


def gradients(frag, block, weights, old_blocks, rights):
    past, rows = len(old_blocks), block.shape[1]
    _, d, cols = weights[0].shape
    spans, at = [], 0
    for right in rights:
        spans.append((at, right.shape[0]))
        at += right.shape[0]
    total = at + rows
    out = pl.pallas_call(
        functools.partial(gradient_kernel, past, tuple(spans)),
        out_shape=[jax.ShapeDtypeStruct((3, d, cols), jnp.bfloat16)] * 2 + [jax.ShapeDtypeStruct((cols, d), jnp.float32)] * 2,
        in_specs=[SMEM] + [ANY] * (past + len(spans) + 3),
        out_specs=[VMEM] * 4,
        scratch_shapes=[
            pltpu.VMEM((rows, d), jnp.bfloat16),
            pltpu.VMEM((rows, d), jnp.bfloat16),
            pltpu.VMEM((rows, cols), jnp.float32),
            pltpu.VMEM((rows, cols), jnp.float32),
            pltpu.VMEM((total, d), jnp.bfloat16),
            pltpu.VMEM((total, 2 * cols), jnp.bfloat16),
            pltpu.SemaphoreType.DMA((past + len(spans) + 9,)),
        ],
        compiler_params=pltpu.CompilerParams(vmem_limit_bytes=20 * MIB),
        cost_estimate=CHEAP,
        name="gradients",
    )(frag, block, *old_blocks, *rights, *weights)
    return out[:2], out[2:]


def step_kernel(count, frag_ref, *refs):
    blocks, (weight, total, out) = refs[:count], refs[count : count + 3]
    n_s, c_s, up_s, dh_s, right_s = refs[count + 3 :]
    rows = blocks[0].shape[1]
    frag = frag_ref[0]
    if count == 1:
        n_s, c_s = blocks[0].at[0], blocks[0].at[1]
    else:
        for k, block in enumerate(blocks):
            n_s[k * rows : (k + 1) * rows, :] = block[0]
            c_s[k * rows : (k + 1) * rows, :] = block[1]
    right_side(frag, Loads(frag, None, 0), 0, n_s, c_s, weight, up_s, dh_s, right_s)
    right_t = right_s[...].T
    pl.when(frag == 2)(functools.partial(add_gradient, right_t, c_s, out, total))
    pl.when(frag != 2)(functools.partial(add_gradient, right_t, n_s, out, total))


def add_blocks(frag, blocks, weight, total, kind=jnp.float32, cost=CHEAP):
    count, rows = len(blocks), len(blocks) * blocks[0].shape[1]
    _, d, cols = weight.shape
    return pl.pallas_call(
        functools.partial(step_kernel, count),
        out_shape=jax.ShapeDtypeStruct((cols, d), kind),
        in_specs=[SMEM] + [VMEM] * (count + 2),
        out_specs=VMEM,
        scratch_shapes=[
            pltpu.VMEM((rows if count > 1 else 16, d), jnp.bfloat16),
            pltpu.VMEM((rows if count > 1 else 16, d), jnp.bfloat16),
            pltpu.VMEM((rows, cols), jnp.float32),
            pltpu.VMEM((rows, cols), jnp.float32),
            pltpu.VMEM((rows, cols), jnp.bfloat16),
        ],
        input_output_aliases={count + 2: 0} if kind == jnp.float32 else {},
        compiler_params=pltpu.CompilerParams(vmem_limit_bytes=12 * MIB),
        cost_estimate=cost,
        name="blocks",
    )(frag, *blocks, weight, total)


def adam_kernel(tokens, tile, own_ref, other_ref, m_ref, v_ref, mixed_ref, out_ref, out_s, sems):
    copies = []
    for i in range(m_ref.shape[0] // tile):
        span = slice(i * tile, (i + 1) * tile)
        grad = (own_ref[:, span] + other_ref[:, span].astype(jnp.float32)).T * (1.0 / tokens)
        moment_one = beta_one * m_ref[span, :] + (1.0 - beta_one) * grad
        moment_two = beta_two * v_ref[span, :] + (1.0 - beta_two) * grad * grad
        root = moment_two * lax.rsqrt(moment_two)
        step_inner = inner_lr * moment_one / (root + adam_eps)
        out_s[span, :] = (mixed_ref[span, :] - mix_alpha * step_inner).astype(jnp.bfloat16)
        copy = pltpu.make_async_copy(out_s.at[span, :], out_ref.at[span, :], sems.at[i])
        copy.start()
        copies.append(copy)
    for copy in copies:
        copy.wait()


def adam(tokens, own, other, m, v, mixed):
    d, cols = m.shape
    tile = 512
    return pl.pallas_call(
        functools.partial(adam_kernel, tokens, tile),
        out_shape=jax.ShapeDtypeStruct((d, cols), jnp.bfloat16),
        in_specs=[VMEM] * 5,
        out_specs=ANY,
        scratch_shapes=[pltpu.VMEM((d, cols), jnp.bfloat16), pltpu.SemaphoreType.DMA((d // tile,))],
        compiler_params=pltpu.CompilerParams(vmem_limit_bytes=12 * MIB),
        cost_estimate=CHEAP,
        name="adam",
    )(own, other, m, v, mixed)


def after(value, *others):
    return lax.optimization_barrier((value, *others))[0]


def per_device(step, hidden_in, cotangent, norm_gain, weights, adam_m, adam_v, global_frag, outer_mom):
    fragment = step[0] % 3
    frag = fragment.reshape(1)
    w_own = weights[0]
    w_sib = lax.ppermute(w_own, "fsdp", SIBLING)
    w_both = [w_sib, w_own]
    own = normed_and_cotangent(hidden_in[0], cotangent[0], norm_gain)

    straight = functools.partial(lax.ppermute, axis_name="fsdp", perm=STRAIGHT)
    crossed = functools.partial(lax.ppermute, axis_name="fsdp", perm=CROSSED)
    other_z = functools.partial(lax.ppermute, axis_name="fsdp", perm=OTHER_Z)

    x = lax.rem(lax.axis_index("replica"), 4)
    first_core = lax.rem(lax.axis_index("fsdp"), 2) == 0
    inner, upper = lax.rem((x + 1) // 2, 2), x // 2
    h = jnp.where(first_core, inner, upper)
    q = jnp.where(first_core, upper, inner)
    everyone = ("replica", "fsdp")
    d, cols = global_frag.shape
    half, quarter = d // 2, d // 4

    def w_rows(at, size):
        return lax.dynamic_slice(w_own, (fragment, at, 0), (1, size, cols))[0]

    def g_rows(at, size):
        return lax.dynamic_slice(global_frag, (at, 0), (size, cols))

    def ordered(second, first, other):
        return jnp.where(second == 0, jnp.concatenate([first, other]), jnp.concatenate([other, first]))

    def wire(value):
        return (value * (WIRE_SCALE / 8)).astype(jnp.float16)

    near = straight(own)
    z_own = other_z(own)
    cross = crossed(own)
    w_pair = lax.ppermute(after(w_rows((1 - h) * half, half), own), everyone, HALF_PAIR)

    def pair_delta(at):
        base = g_rows(h * half + at, quarter)
        mine = w_rows(h * half + at, quarter).astype(jnp.float32)
        theirs = lax.dynamic_slice_in_dim(w_pair, at, quarter).astype(jnp.float32)
        return (base - mine) + (base - theirs)

    sent = wire(pair_delta((1 - q) * quarter))
    got = lax.ppermute(sent, everyone, QUARTER_PAIR)
    part = wire(pair_delta(q * quarter) + got.astype(jnp.float32) * (8 / WIRE_SCALE))
    z_own, near, part = lax.optimization_barrier((z_own, near, part))
    other = lax.ppermute(part, "replica", OTHER_H)
    z_near = straight(z_own)
    far = straight(near)
    first = [own, near, cross, z_own]
    right = forward(frag, first, w_both)
    other = after(other, right)
    mine = (part.astype(jnp.float32) + other.astype(jnp.float32)).astype(jnp.float16)
    cross, mine = lax.optimization_barrier((cross, mine))
    z_cross = other_z(cross)
    beside, across = lax.ppermute(mine, everyone, QUARTER_PAIR), lax.ppermute(mine, everyone, HALF_PAIR)
    opposite = lax.ppermute(mine, "replica", OPPOSITE)
    rights = [right, forward(frag, [z_near], w_both)]
    z_far = straight(after(z_near, beside, rights[1]))

    delta = ordered(h, ordered(q, mine, beside), ordered(q, across, opposite)).astype(jnp.float32) * (1 / WIRE_SCALE)
    momentum_new = nesterov_mu * outer_mom + delta
    global_new = global_frag - outer_lr * (delta + nesterov_mu * momentum_new)
    mixed = mix_alpha * w_rows(0, d).astype(jnp.float32) + (1.0 - mix_alpha) * global_new

    held, totals = gradients(frag, far, w_both, [*first, z_near], [rights[0], after(rights[1], mixed)])
    cost = pl.CostEstimate(flops=8 * z_cross.size * cols, bytes_accessed=3 * totals[0].size * 4, transcendentals=0)
    sib_total = add_blocks(frag, [z_cross], held[0], totals[0], cost=cost)
    grad_sib = add_blocks(frag, [z_far], held[0], sib_total, jnp.bfloat16)
    grad_sib = lax.ppermute(grad_sib, "fsdp", SIBLING)
    grad_own = add_blocks(frag, [z_cross, z_far], held[1], totals[1])
    tokens_total = hidden_in.shape[1] * lax.axis_size("fsdp")
    merged = adam(tokens_total, grad_own, grad_sib, adam_m[0], adam_v[0], mixed)
    return (global_new, momentum_new, merged[None])


def solution(mesh):
    placed = (
        P(),
        P("replica", "fsdp", None),
        P("replica", "fsdp", None),
        P(),
        P("replica", None, None, "fsdp"),
        P("replica", None, "fsdp"),
        P("replica", None, "fsdp"),
        P(None, "fsdp"),
        P(None, "fsdp"),
    )
    return jax.shard_map(
        per_device,
        mesh=mesh,
        in_specs=placed,
        out_specs=(P(None, "fsdp"), P(None, "fsdp"), P("replica", None, "fsdp")),
        check_vma=False,
    )
```

```python
import functools

import jax
import jax.numpy as jnp
from jax import lax
from jax.experimental import pallas as pl
from jax.experimental.pallas import tpu as pltpu
from jax.sharding import PartitionSpec as P

beta_one = 0.9
beta_two = 0.95
adam_eps = 1e-08
inner_lr = 0.02
outer_lr = 0.7
nesterov_mu = 0.9
mix_alpha = 0.5
norm_eps = 1e-05

WIRE_SCALE = float(2**18)

ANY = pl.BlockSpec(memory_space=pl.ANY)
VMEM = pl.BlockSpec(memory_space=pltpu.VMEM)
SMEM = pl.BlockSpec(memory_space=pltpu.SMEM)
MIB = 1024 * 1024
CHEAP = pl.CostEstimate(flops=1, bytes_accessed=1, transcendentals=0)


def fsdp_id(z, y, c):
    return (z % 2) * 8 + (y % 4) * 2 + c


def permutation(to):
    return [(fsdp_id(z, y, c), fsdp_id(*to(z, y, c))) for z in range(2) for y in range(4) for c in range(2)]


STRAIGHT = permutation(lambda z, y, c: (z, y + 1 - 2 * c, c))
CROSSED = permutation(lambda z, y, c: (z, y + 2 * c - 1, 1 - c))
OTHER_Z = permutation(lambda z, y, c: (z + 1, y, c))
SIBLING = permutation(lambda z, y, c: (z, y, 1 - c))


def replica_pairs(first):
    pairs = []
    for r in range(8):
        for i in range(16):
            beside = (r % 4) ^ 1 if (i % 2 == 0) == first else 3 - r % 4
            pairs.append((r * 16 + i, (r // 4 * 4 + beside) * 16 + i))
    return pairs


HALF_PAIR = replica_pairs(True)
QUARTER_PAIR = replica_pairs(False)
OPPOSITE = [(r, r // 4 * 4 + (r + 2) % 4) for r in range(8)]
OTHER_H = [(r, (r + 4) % 8) for r in range(8)]


def norm_kernel(x_ref, c_ref, g_ref, u_ref, x_s, g_s, sems):
    g_in = pltpu.make_async_copy(g_ref, g_s, sems.at[0])
    c_in = pltpu.make_async_copy(c_ref, u_ref.at[1], sems.at[1])
    tile = x_ref.shape[0] // 2
    spans = [pl.ds(0, tile), pl.ds(tile, tile)]
    x_in = [pltpu.make_async_copy(x_ref.at[span], x_s.at[span], sems.at[2 + i]) for i, span in enumerate(spans)]
    for copy in (g_in, *x_in, c_in):
        copy.start()
    g_in.wait()
    gain = g_s[...].astype(jnp.float32).reshape(1, -1)
    for span, copy in zip(spans, x_in):
        copy.wait()
        x = x_s[span].astype(jnp.float32)
        scale = lax.rsqrt(jnp.mean(x * x, axis=1, keepdims=True) + norm_eps)
        u_ref[0, span] = (x * scale * gain).astype(jnp.bfloat16)
    c_in.wait()


def normed_and_cotangent(x, c, gain):
    return pl.pallas_call(
        norm_kernel,
        out_shape=jax.ShapeDtypeStruct((2, *x.shape), jnp.bfloat16),
        in_specs=[ANY, ANY, ANY],
        out_specs=VMEM,
        scratch_shapes=[
            pltpu.VMEM(x.shape, jnp.bfloat16),
            pltpu.VMEM(gain.shape, jnp.bfloat16),
            pltpu.SemaphoreType.DMA((4,)),
        ],
        compiler_params=pltpu.CompilerParams(vmem_limit_bytes=60 * MIB),
        cost_estimate=CHEAP,
        name="norm",
    )(x, c, gain)


class Loads:
    def __init__(self, frag, sems, ahead):
        self.frag, self.sems, self.ahead = frag, sems, ahead
        self.entries, self.started, self.waited = [], 0, 0

    def add(self, name, source, target, without=None):
        copy = pltpu.make_async_copy(source, target, self.sems.at[len(self.entries)])
        self.entries.append((name, copy, without))

    def unless(self, without, act):
        if without is None:
            act()
        else:
            pl.when(self.frag != without)(act)

    def start(self):
        while self.started < min(self.waited + self.ahead, len(self.entries)):
            _, copy, without = self.entries[self.started]
            self.unless(without, copy.start)
            self.started += 1

    def wait(self, name):
        while self.waited < len(self.entries) and self.entries[self.waited][0] == name:
            _, copy, without = self.entries[self.waited]
            self.unless(without, copy.wait)
            self.waited += 1
            self.start()


def right_side(frag, loads, tag, n_s, c_s, w_s, up_s, dh_s, right):
    def dot(left, i):
        return jnp.dot(left[...], w_s[i], preferred_element_type=jnp.float32)

    loads.wait(("n", tag))
    loads.wait(("gate", tag))
    gate = dot(n_s, 0)
    loads.wait(("up", tag))

    @pl.when(frag != 1)
    def _():
        up_s[...] = dot(n_s, 1)

    loads.wait(("c", tag))
    loads.wait(("down", tag))

    @pl.when(frag != 2)
    def _():
        dh_s[...] = dot(c_s, 2)

    sig = jax.nn.sigmoid(gate)

    @pl.when(frag == 0)
    def _():
        right[...] = (dh_s[...] * up_s[...] * sig * (1.0 + gate * (1.0 - sig))).astype(jnp.bfloat16)

    @pl.when(frag == 1)
    def _():
        right[...] = (dh_s[...] * (gate * sig)).astype(jnp.bfloat16)

    @pl.when(frag == 2)
    def _():
        right[...] = (gate * sig * up_s[...]).astype(jnp.bfloat16)


def forward_kernel(count, frag_ref, *refs):
    blocks, weights, out_ref = refs[:count], refs[count : count + 2], refs[count + 2]
    n_s, c_s, w_s, up_s, dh_s, sems = refs[count + 3 :]
    rows, cols = blocks[0].shape[1], weights[0].shape[2]
    frag = frag_ref[0]
    loads = Loads(frag, sems, count + 4)
    for h, weight in enumerate(weights):
        if h == 0:
            for k, b in enumerate(blocks):
                loads.add(("n", h), b.at[0], n_s.at[pl.ds(k * rows, rows)])
        loads.add(("gate", h), weight.at[0], w_s.at[h, 0])
        loads.add(("up", h), weight.at[1], w_s.at[h, 1], 1)
        if h == 0:
            for k, b in enumerate(blocks):
                loads.add(("c", h), b.at[1], c_s.at[pl.ds(k * rows, rows)], 2)
        loads.add(("down", h), weight.at[2], w_s.at[h, 2], 2)
    loads.start()
    for h in range(2):
        right = out_ref.at[:, h * cols : (h + 1) * cols]
        right_side(frag, loads, h, n_s, c_s, w_s.at[h], up_s, dh_s, right)


def forward(frag, blocks, weights):
    count, rows = len(blocks), len(blocks) * blocks[0].shape[1]
    _, d, cols = weights[0].shape
    return pl.pallas_call(
        functools.partial(forward_kernel, count),
        out_shape=jax.ShapeDtypeStruct((rows, 2 * cols), jnp.bfloat16),
        in_specs=[SMEM] + [ANY] * (count + 2),
        out_specs=VMEM,
        scratch_shapes=[
            pltpu.VMEM((rows, d), jnp.bfloat16),
            pltpu.VMEM((rows, d), jnp.bfloat16),
            pltpu.VMEM((2, 3, d, cols), jnp.bfloat16),
            pltpu.VMEM((rows, cols), jnp.float32),
            pltpu.VMEM((rows, cols), jnp.float32),
            pltpu.SemaphoreType.DMA((2 * count + 6,)),
        ],
        compiler_params=pltpu.CompilerParams(vmem_limit_bytes=60 * MIB),
        cost_estimate=CHEAP,
        name="forward",
    )(frag, *blocks, *weights)


def add_gradient(right_t, left, out, total=None):
    step = 768
    for at in range(0, out.shape[1], step):
        span = slice(at, at + step)
        term = jnp.dot(right_t, left[:, span], preferred_element_type=jnp.float32)
        if total is not None:
            term = total[:, span] + term
        out[:, span] = term.astype(out.dtype)


def gradient_kernel(past, spans, frag_ref, block, *refs):
    old_blocks, rights, refs = refs[:past], refs[past : past + len(spans)], refs[past + len(spans) :]
    weights, held, outs = refs[:2], refs[2:4], refs[4:6]
    n_s, c_s, up_s, dh_s, left_s, right_s, sems = refs[6:]
    rows, cols = block.shape[1], weights[0].shape[2]
    frag = frag_ref[0]
    side = jnp.where(frag == 2, 1, 0)
    loads = Loads(frag, sems, 8)
    for h in range(2):
        if h == 0:
            loads.add(("n", h), block.at[0], n_s)
        loads.add(("gate", h), weights[h].at[0], held[h].at[0])
        loads.add(("up", h), weights[h].at[1], held[h].at[1], 1)
        if h == 0:
            loads.add(("c", h), block.at[1], c_s)
        loads.add(("down", h), weights[h].at[2], held[h].at[2], 2)
        if h == 0:
            for right, (at, size) in zip(rights, spans):
                loads.add("rest", right, right_s.at[pl.ds(at, size)])
            for k, b in enumerate((*old_blocks, block)):
                loads.add("rest", b.at[side], left_s.at[pl.ds(k * rows, rows)])
    loads.start()
    for h in range(2):
        here = slice(h * cols, (h + 1) * cols)
        right_side(frag, loads, h, n_s, c_s, held[h], up_s, dh_s, right_s.at[past * rows :, here])
        loads.wait("rest")
        add_gradient(right_s[:, here].T, left_s, outs[h])


def gradients(frag, block, weights, old_blocks, rights):
    past, rows = len(old_blocks), block.shape[1]
    _, d, cols = weights[0].shape
    spans, at = [], 0
    for right in rights:
        spans.append((at, right.shape[0]))
        at += right.shape[0]
    total = at + rows
    out = pl.pallas_call(
        functools.partial(gradient_kernel, past, tuple(spans)),
        out_shape=[jax.ShapeDtypeStruct((3, d, cols), jnp.bfloat16)] * 2 + [jax.ShapeDtypeStruct((cols, d), jnp.float32)] * 2,
        in_specs=[SMEM] + [ANY] * (past + len(spans) + 3),
        out_specs=[VMEM] * 4,
        scratch_shapes=[
            pltpu.VMEM((rows, d), jnp.bfloat16),
            pltpu.VMEM((rows, d), jnp.bfloat16),
            pltpu.VMEM((rows, cols), jnp.float32),
            pltpu.VMEM((rows, cols), jnp.float32),
            pltpu.VMEM((total, d), jnp.bfloat16),
            pltpu.VMEM((total, 2 * cols), jnp.bfloat16),
            pltpu.SemaphoreType.DMA((past + len(spans) + 9,)),
        ],
        compiler_params=pltpu.CompilerParams(vmem_limit_bytes=20 * MIB),
        cost_estimate=CHEAP,
        name="gradients",
    )(frag, block, *old_blocks, *rights, *weights)
    return out[:2], out[2:]


def step_kernel(count, frag_ref, *refs):
    blocks, (weight, total, out) = refs[:count], refs[count : count + 3]
    n_s, c_s, up_s, dh_s, right_s = refs[count + 3 :]
    rows = blocks[0].shape[1]
    frag = frag_ref[0]
    if count == 1:
        n_s, c_s = blocks[0].at[0], blocks[0].at[1]
    else:
        for k, block in enumerate(blocks):
            n_s[k * rows : (k + 1) * rows, :] = block[0]
            c_s[k * rows : (k + 1) * rows, :] = block[1]
    right_side(frag, Loads(frag, None, 0), 0, n_s, c_s, weight, up_s, dh_s, right_s)
    right_t = right_s[...].T
    pl.when(frag == 2)(functools.partial(add_gradient, right_t, c_s, out, total))
    pl.when(frag != 2)(functools.partial(add_gradient, right_t, n_s, out, total))


def add_blocks(frag, blocks, weight, total, kind=jnp.float32, cost=CHEAP):
    count, rows = len(blocks), len(blocks) * blocks[0].shape[1]
    _, d, cols = weight.shape
    return pl.pallas_call(
        functools.partial(step_kernel, count),
        out_shape=jax.ShapeDtypeStruct((cols, d), kind),
        in_specs=[SMEM] + [VMEM] * (count + 2),
        out_specs=VMEM,
        scratch_shapes=[
            pltpu.VMEM((rows if count > 1 else 16, d), jnp.bfloat16),
            pltpu.VMEM((rows if count > 1 else 16, d), jnp.bfloat16),
            pltpu.VMEM((rows, cols), jnp.float32),
            pltpu.VMEM((rows, cols), jnp.float32),
            pltpu.VMEM((rows, cols), jnp.bfloat16),
        ],
        input_output_aliases={count + 2: 0} if kind == jnp.float32 else {},
        compiler_params=pltpu.CompilerParams(vmem_limit_bytes=12 * MIB),
        cost_estimate=cost,
        name="blocks",
    )(frag, *blocks, weight, total)


def right_kernel(frag_ref, block, weight, out_ref, up_s, dh_s):
    frag = frag_ref[0]
    right_side(frag, Loads(frag, None, 0), 0, block.at[0], block.at[1], weight, up_s, dh_s, out_ref)


def right_of(frag, block, weight, cost):
    rows, cols = block.shape[1], weight.shape[2]
    return pl.pallas_call(
        right_kernel,
        out_shape=jax.ShapeDtypeStruct((rows, cols), jnp.bfloat16),
        in_specs=[SMEM, VMEM, VMEM],
        out_specs=VMEM,
        scratch_shapes=[pltpu.VMEM((rows, cols), jnp.float32)] * 2,
        compiler_params=pltpu.CompilerParams(vmem_limit_bytes=12 * MIB),
        cost_estimate=cost,
        name="right",
    )(frag, block, weight)


def last_kernel(frag_ref, block, past, past_right, weight, total, out, up_s, dh_s, right_s):
    rows = block.shape[1]
    frag = frag_ref[0]
    right_s[:rows, :] = past_right[...]
    right_side(frag, Loads(frag, None, 0), 0, block.at[0], block.at[1], weight, up_s, dh_s, right_s.at[rows:, :])
    right_t = right_s[...].T

    def add(side):
        step = 768
        for at in range(0, out.shape[1], step):
            span = slice(at, at + step)
            left = jnp.concatenate([past[side, :, span], block[side, :, span]], axis=0)
            term = total[:, span] + jnp.dot(right_t, left, preferred_element_type=jnp.float32)
            out[:, span] = term.astype(out.dtype)

    pl.when(frag == 2)(lambda: add(1))
    pl.when(frag != 2)(lambda: add(0))


def last_gradient(frag, block, past, past_right, weight, total):
    rows = block.shape[1]
    _, d, cols = weight.shape
    return pl.pallas_call(
        last_kernel,
        out_shape=jax.ShapeDtypeStruct((cols, d), jnp.bfloat16),
        in_specs=[SMEM] + [VMEM] * 5,
        out_specs=VMEM,
        scratch_shapes=[pltpu.VMEM((rows, cols), jnp.float32)] * 2 + [pltpu.VMEM((2 * rows, cols), jnp.bfloat16)],
        compiler_params=pltpu.CompilerParams(vmem_limit_bytes=12 * MIB),
        cost_estimate=CHEAP,
        name="last",
    )(frag, block, past, past_right, weight, total)


def adam_kernel(tokens, tile, own_ref, other_ref, m_ref, v_ref, mixed_ref, out_ref, out_s, sems):
    copies = []
    for i in range(m_ref.shape[0] // tile):
        span = slice(i * tile, (i + 1) * tile)
        grad = (own_ref[:, span] + other_ref[:, span].astype(jnp.float32)).T * (1.0 / tokens)
        moment_one = beta_one * m_ref[span, :] + (1.0 - beta_one) * grad
        moment_two = beta_two * v_ref[span, :] + (1.0 - beta_two) * grad * grad
        root = moment_two * lax.rsqrt(moment_two)
        step_inner = inner_lr * moment_one / (root + adam_eps)
        out_s[span, :] = (mixed_ref[span, :] - mix_alpha * step_inner).astype(jnp.bfloat16)
        copy = pltpu.make_async_copy(out_s.at[span, :], out_ref.at[span, :], sems.at[i])
        copy.start()
        copies.append(copy)
    for copy in copies:
        copy.wait()


def adam(tokens, own, other, m, v, mixed):
    d, cols = m.shape
    tile = 512
    return pl.pallas_call(
        functools.partial(adam_kernel, tokens, tile),
        out_shape=jax.ShapeDtypeStruct((d, cols), jnp.bfloat16),
        in_specs=[VMEM] * 5,
        out_specs=ANY,
        scratch_shapes=[pltpu.VMEM((d, cols), jnp.bfloat16), pltpu.SemaphoreType.DMA((d // tile,))],
        compiler_params=pltpu.CompilerParams(vmem_limit_bytes=12 * MIB),
        cost_estimate=CHEAP,
        name="adam",
    )(own, other, m, v, mixed)


def after(value, *others):
    return lax.optimization_barrier((value, *others))[0]


def per_device(step, hidden_in, cotangent, norm_gain, weights, adam_m, adam_v, global_frag, outer_mom):
    fragment = step[0] % 3
    frag = fragment.reshape(1)
    w_own = weights[0]
    w_sib = lax.ppermute(w_own, "fsdp", SIBLING)
    w_both = [w_sib, w_own]
    own = normed_and_cotangent(hidden_in[0], cotangent[0], norm_gain)

    straight = functools.partial(lax.ppermute, axis_name="fsdp", perm=STRAIGHT)
    crossed = functools.partial(lax.ppermute, axis_name="fsdp", perm=CROSSED)
    other_z = functools.partial(lax.ppermute, axis_name="fsdp", perm=OTHER_Z)

    x = lax.rem(lax.axis_index("replica"), 4)
    first_core = lax.rem(lax.axis_index("fsdp"), 2) == 0
    inner, upper = lax.rem((x + 1) // 2, 2), x // 2
    h = jnp.where(first_core, inner, upper)
    q = jnp.where(first_core, upper, inner)
    everyone = ("replica", "fsdp")
    d, cols = global_frag.shape
    half, quarter = d // 2, d // 4

    def w_rows(at, size):
        return lax.dynamic_slice(w_own, (fragment, at, 0), (1, size, cols))[0]

    def g_rows(at, size):
        return lax.dynamic_slice(global_frag, (at, 0), (size, cols))

    def ordered(second, first, other):
        return jnp.where(second == 0, jnp.concatenate([first, other]), jnp.concatenate([other, first]))

    def wire(value):
        return (value * (WIRE_SCALE / 8)).astype(jnp.float16)

    near = straight(own)
    z_own = other_z(own)
    cross = crossed(own)
    w_pair = lax.ppermute(after(w_rows((1 - h) * half, half), own), everyone, HALF_PAIR)

    def pair_delta(at):
        base = g_rows(h * half + at, quarter)
        mine = w_rows(h * half + at, quarter).astype(jnp.float32)
        theirs = lax.dynamic_slice_in_dim(w_pair, at, quarter).astype(jnp.float32)
        return (base - mine) + (base - theirs)

    sent = wire(pair_delta((1 - q) * quarter))
    got = lax.ppermute(sent, everyone, QUARTER_PAIR)
    part = wire(pair_delta(q * quarter) + got.astype(jnp.float32) * (8 / WIRE_SCALE))
    z_own, near, part = lax.optimization_barrier((z_own, near, part))
    other = lax.ppermute(part, "replica", OTHER_H)
    z_near = straight(z_own)
    far = straight(near)
    first = [own, near, cross, z_own]
    right = forward(frag, first, w_both)
    other = after(other, right)
    mine = (part.astype(jnp.float32) + other.astype(jnp.float32)).astype(jnp.float16)
    cross, mine = lax.optimization_barrier((cross, mine))
    z_cross = other_z(cross)
    beside, across = lax.ppermute(mine, everyone, QUARTER_PAIR), lax.ppermute(mine, everyone, HALF_PAIR)
    opposite = lax.ppermute(mine, "replica", OPPOSITE)
    rights = [right, forward(frag, [z_near], w_both)]
    z_far = straight(after(z_near, beside, rights[1]))

    delta = ordered(h, ordered(q, mine, beside), ordered(q, across, opposite)).astype(jnp.float32) * (1 / WIRE_SCALE)
    momentum_new = nesterov_mu * outer_mom + delta
    global_new = global_frag - outer_lr * (delta + nesterov_mu * momentum_new)
    mixed = mix_alpha * w_rows(0, d).astype(jnp.float32) + (1.0 - mix_alpha) * global_new

    held, totals = gradients(frag, far, w_both, [*first, z_near], [rights[0], after(rights[1], mixed)])
    cost = pl.CostEstimate(flops=8 * z_cross.size * cols, bytes_accessed=3 * totals[0].size * 4, transcendentals=0)
    right_cross = right_of(frag, z_cross, held[0], cost)
    grad_sib = last_gradient(frag, z_far, z_cross, right_cross, held[0], totals[0])
    grad_sib = lax.ppermute(grad_sib, "fsdp", SIBLING)
    grad_own = add_blocks(frag, [z_cross, z_far], held[1], totals[1])
    tokens_total = hidden_in.shape[1] * lax.axis_size("fsdp")
    merged = adam(tokens_total, grad_own, grad_sib, adam_m[0], adam_v[0], mixed)
    return (global_new, momentum_new, merged[None])


def solution(mesh):
    placed = (
        P(),
        P("replica", "fsdp", None),
        P("replica", "fsdp", None),
        P(),
        P("replica", None, None, "fsdp"),
        P("replica", None, "fsdp"),
        P("replica", None, "fsdp"),
        P(None, "fsdp"),
        P(None, "fsdp"),
    )
    return jax.shard_map(
        per_device,
        mesh=mesh,
        in_specs=placed,
        out_specs=(P(None, "fsdp"), P(None, "fsdp"), P("replica", None, "fsdp")),
        check_vma=False,
    )
```
